32 devices in a mesh: space: 8 (over y, x, core), sample: 4 (over z).
Axes of the slice: x: 2, y: 2, z: 4, core: 2. Of those that a mesh axis runs over, the one named last changes fastest.
Arguments:
- ensemble: bfloat16 [48, 4, 1024, 1024], P(None, 'sample', 'space'), may hold values from -6 to 6
- map_one: bfloat16 [1024, 256], P('space'), may hold values from -0.1875 to 0.1875
- map_two: bfloat16 [1024, 256], replicated, may hold values from -0.1875 to 0.1875
- map_three: bfloat16 [48, 256], replicated, may hold values from -0.875 to 0.875
- map_four: bfloat16 [4, 256], P('sample'), may hold values from -3 to 3
- core_one: bfloat16 [1024, 128], replicated, may hold values from -0.1875 to 0.1875
- core_two: bfloat16 [1024, 128], replicated, may hold values from -0.1875 to 0.1875
- core_three: bfloat16 [48, 128], replicated, may hold values from -0.875 to 0.875
- core_four: bfloat16 [4, 128], replicated, may hold values from -3 to 3
Outputs:
- sketch_one: float32 [1024, 256], P('space', 'sample')
- sketch_two: float32 [1024, 256], P(('space', 'sample'))
- sketch_three: float32 [48, 256], replicated
- sketch_four: float32 [4, 256], P('sample')
- core_sketch: float32 [128, 16384, 128], P(None, ('space', 'sample'))
The draws below stay inside these ranges and needn't reach their ends.
All inputs are finite; a program needn't handle non-finite values.
Results may differ from the reference program's by a relative error of at most 0.0029.
Values sent between devices are 32-bit elements; how exact they have to be, the bound alone decides.
No kernel may reach another device: no remote copies, remote signals or barrier semaphores. Data moves between devices by JAX's collectives and lax.ppermute only.
A program may use at most 128 MiB of HBM per device.

```python
import jax
import jax.numpy as jnp
from jax import lax

N1 = 1024
N2 = 1024
K = 256
R = 128
TS = 16
SLABS = 3
TT = 48
NS = 4


def strengthened(entries, rng, source, target, shards_of, factor):
    owner, partner = [(jnp.arange(entries.shape[axis_at]) // (entries.shape[axis_at] // shards_of)).reshape([-1 if axis == axis_at else 1 for axis in range(entries.ndim)]) for axis_at in (source, target)]
    chosen = jax.random.permutation(rng, shards_of)[partner]
    strong = (owner == chosen) | (owner == (partner + shards_of // 2) % shards_of)
    return jnp.where(strong, factor * entries, entries)


def levels(key, dims, cuts, smallest, top_value):
    def one(position, parts):
        heights = jax.random.uniform(jax.random.fold_in(jax.random.fold_in(key, 6), position), (parts,), jnp.float32, smallest / len(cuts), top_value / len(cuts))
        return jnp.repeat(jnp.exp(heights), dims[position] // parts).reshape((-1,) + (1,) * (len(dims) - position - 1))

    gain = one(*cuts[0])
    for cut in cuts[1:]:
        gain = gain * one(*cut)
    return gain


def noise(rng, shape, spread, bound, shards=(), dtype=jnp.bfloat16):
    values = jax.random.normal(rng, shape, jnp.float32) * spread
    if len(shards) > 0:
        values = levels(rng, shape, shards, -0.22, 0.18) * values
    return jnp.clip(values, min=-bound, max=bound).astype(dtype)


def heavy_noise(key, extent, scale, most, split, heavy, dtype=jnp.bfloat16):
    entries = scale * jax.random.normal(key, extent, jnp.float32)
    if split:
        entries = entries * levels(key, extent, split, -0.22, 0.18)
    return jnp.clip(strengthened(entries, jax.random.fold_in(key, 3), *heavy), -most, most).astype(dtype)


def setup_inputs(seed: int = 0) -> dict:
    seeds = jax.random.split(jax.random.key(seed), 10)
    ensemble = heavy_noise(seeds[0], (TT, NS, N1, N2), 1.0, 6.0, ((1, 4), (2, 8)), (2, 3, 8, 2.0))
    map_one = noise(seeds[1], (N1, K), N1 ** -0.5, 0.1875, ((0, 8),))
    map_two = noise(seeds[2], (N2, K), N2 ** -0.5, 0.1875)
    map_three = noise(seeds[3], (TT, K), TT ** -0.5, 0.875)
    map_four = noise(seeds[4], (NS, K), NS ** -0.5, 3.0, ((0, 4),))
    core_one = noise(seeds[5], (N1, R), N1 ** -0.5, 0.1875)
    core_two = noise(seeds[6], (N2, R), N2 ** -0.5, 0.1875)
    core_three = noise(seeds[7], (TT, R), TT ** -0.5, 0.875)
    core_four = noise(seeds[8], (NS, R), NS ** -0.5, 3.0)
    return {"ensemble": ensemble, "map_one": map_one, "map_two": map_two, "map_three": map_three, "map_four": map_four, "core_one": core_one, "core_two": core_two, "core_three": core_three, "core_four": core_four}


def reference(ensemble, map_one, map_two, map_three, map_four, core_one, core_two, core_three, core_four):
    high = lax.Precision.HIGHEST
    joined = jnp.concatenate([map_two, core_two], axis=1)
    rows_one = map_one.astype(jnp.float32)
    rows_four = map_four.astype(jnp.float32)
    phi_one = core_one.astype(jnp.float32)
    phi_four = core_four.astype(jnp.float32)
    sketch_one = jnp.zeros((N1, K), jnp.float32)
    sketch_two = jnp.zeros((N2, K), jnp.float32)
    sketch_four = jnp.zeros((NS, K), jnp.float32)
    core = jnp.zeros((R, R, R, R), jnp.float32)
    thirds = []
    for index in range(SLABS):
        block = ensemble[index * TS:(index + 1) * TS]
        flat = block.reshape(-1, N2)
        both = jnp.dot(flat, joined, preferred_element_type=jnp.float32)
        proj = both[:, :K].reshape(TS, NS, N1, K)
        cproj = both[:, K:].reshape(TS, NS, N1, R)
        third = map_three[index * TS:(index + 1) * TS].astype(jnp.float32)
        time_core = core_three[index * TS:(index + 1) * TS].astype(jnp.float32)
        pair_ts = third[:, None, :] * rows_four[None, :, :]
        pair_si = rows_four[:, None, :] * rows_one[None, :, :]
        pair_ti = third[:, None, :] * rows_one[None, :, :]
        sketch_one = sketch_one + jnp.einsum('tsik,tsk->ik', proj, pair_ts, precision=high)
        thirds.append(jnp.einsum('tsik,sik->tk', proj, pair_si, precision=high))
        sketch_four = sketch_four + jnp.einsum('tsik,tik->sk', proj, pair_ti, precision=high)
        krao = (pair_ts[:, :, None, :] * rows_one[None, None, :, :]).astype(jnp.bfloat16).reshape(-1, K)
        sketch_two = sketch_two + jnp.dot(flat.T, krao, preferred_element_type=jnp.float32)
        half = jnp.einsum('tsib,ia->tsab', cproj, phi_one, precision=high)
        quarter = jnp.einsum('tsab,sd->tdab', half, phi_four, precision=high)
        core = core + jnp.einsum('tdab,tc->abcd', quarter, time_core, precision=high)
    sketch_three = jnp.concatenate(thirds, axis=0)
    return sketch_one, sketch_two, sketch_three, sketch_four, core.reshape(R, R * R, R)
```

```python
import functools

import jax
import jax.numpy as jnp
from jax import lax
from jax.experimental import pallas as pl
from jax.experimental.pallas import tpu as pltpu
from jax.sharding import PartitionSpec as P

BF16 = jnp.bfloat16
F32 = jnp.float32
NT = (((1,), (1,)), ((), ()))
MIB = 1 << 20


def split(value):
    high = value.astype(BF16)
    return high, (value - high.astype(F32)).astype(BF16)


def core_kernel(
    space, sample, block, x_ref, two_ref, one_ref, keep_ref, send_ref, left_ref, right_ref
):
    step = pl.program_id(0)
    points, rank = x_ref.shape[2], two_ref.shape[1]
    half = rank // 2
    times = keep_ref.shape[0] // half

    @pl.when(step == 0)
    def _():
        me, my = lax.axis_index("space"), lax.axis_index("sample")
        own = rank // (space * sample)
        slot = lax.broadcasted_iota(jnp.int32, (rank, rank), 0)
        column = lax.broadcasted_iota(jnp.int32, (rank, rank), 1)
        odd = slot // half
        rest = slot % half
        inner = rest % own
        far = (rest // own) % sample
        chip = rest // (own * sample)
        place = ((chip * 2 + odd) ^ me) * sample + (far ^ my)
        pick = jnp.where(column == place * own + inner, 1.0, 0.0).astype(BF16)
        left_ref[...] = lax.dot_general(
            pick, two_ref[...], NT, preferred_element_type=F32
        ).astype(BF16)
        groups = sample
        wide = rank // groups
        row = lax.broadcasted_iota(jnp.int32, (rank, rank), 0)
        group, within = column // wide, column % wide
        source = (within // 2) * (2 * groups) + 2 * group + within % 2
        order = jnp.where(row == source, 1.0, 0.0).astype(BF16)
        mine = one_ref[pl.ds(pl.multiple_of(me * points, points), points), :]
        ordered = jnp.dot(mine, order, preferred_element_type=F32).astype(BF16)
        right_ref[...] = jnp.concatenate([ordered, ordered], axis=0)

    x = x_ref[...].reshape(block * points, x_ref.shape[3])
    first = lax.dot_general(left_ref[...], x, NT, preferred_element_type=F32)
    rows = []
    for t in range(block):
        high, low = split(first[:, t * points : (t + 1) * points])
        rows.append(jnp.concatenate([high, low], axis=1))
    out = jnp.dot(
        jnp.concatenate(rows, axis=0), right_ref[...], preferred_element_type=F32
    )
    for t in range(block):
        at = step * block + t
        keep_ref[pl.ds(at, half, stride=times), :] = out[t * rank : t * rank + half]
        send_ref[pl.ds(at, half, stride=times), :] = out[t * rank + half : (t + 1) * rank]


def core_partial(ensemble, core_one, core_two, space, sample, block):
    times, _, points, width = ensemble.shape
    rank = core_two.shape[1]
    shape = jax.ShapeDtypeStruct((rank // 2 * times, rank), F32)
    whole = lambda i: (0, 0)
    return pl.pallas_call(
        functools.partial(core_kernel, space, sample, block),
        grid=(times // block,),
        in_specs=[
            pl.BlockSpec((block, 1, points, width), lambda i: (i, 0, 0, 0)),
            pl.BlockSpec(core_two.shape, whole),
            pl.BlockSpec(core_one.shape, whole),
        ],
        out_specs=[pl.BlockSpec(shape.shape, whole)] * 2,
        out_shape=[shape, shape],
        scratch_shapes=[
            pltpu.VMEM((rank, width), BF16),
            pltpu.VMEM((2 * points, rank), BF16),
        ],
        compiler_params=pltpu.CompilerParams(vmem_limit_bytes=24 * MIB),
        cost_estimate=pl.CostEstimate(
            flops=2 * ensemble.size * rank, bytes_accessed=2 * ensemble.size, transcendentals=0
        ),
        name="core_partial",
    )(ensemble, core_two, core_one)


def sketch_kernel(
    space, sample, block, x_ref, one_ref, two_ref, three_ref, four_ref,
    keep_ref, send_ref, first_ref,
    acc_one, acc_two, acc_u, pairs, rolled, one_t, turned,
):
    step = pl.program_id(0)
    points, width = x_ref.shape[2], two_ref.shape[1]
    times = three_ref.shape[0]
    cols = x_ref.shape[3]

    @pl.when(step == 0)
    def _():
        acc_one[...] = jnp.zeros_like(acc_one)
        acc_two[...] = jnp.zeros_like(acc_two)
        four = four_ref[...].astype(F32)
        pair = three_ref[...].astype(F32) * four
        pairs[...] = pair.reshape(pairs.shape)
        padded = jnp.concatenate([pair, jnp.zeros((128 - times, width), F32)], axis=0)
        flipped = padded.T
        for n in range(times // block):
            rolled[n] = pltpu.roll(flipped, (128 - n * block) % 128, 1)
        one = one_ref[...].astype(F32)
        if points < 128:
            one = jnp.concatenate([one, jnp.zeros((128 - points, width), F32)], axis=0)
        one_t[...] = one.T[:, :points]

    x = x_ref[...].reshape(block * points, cols)
    proj = jnp.dot(x, two_ref[...], preferred_element_type=F32)
    one = one_ref[...].astype(F32)
    weights = rolled[step]
    total = acc_one[...]
    sums, krao = [], []
    for t in range(block):
        part = proj[t * points : (t + 1) * points]
        total = total + part * pairs[step, t : t + 1, :]
        sums.append(jnp.sum(part * one, axis=0, keepdims=True))
        krao.append((weights[:, t : t + 1] * one_t[...]).astype(BF16))
    acc_one[...] = total
    acc_u[step] = jnp.concatenate(sums, axis=0)
    acc_two[...] += jnp.dot(
        jnp.concatenate(krao, axis=1), x, preferred_element_type=F32
    )

    @pl.when(step == pl.num_programs(0) - 1)
    def _():
        me, my = lax.axis_index("space"), lax.axis_index("sample")
        turned[...] = acc_two[...].T
        own = cols // (space * sample)
        for slot in range(space):
            ref = send_ref if slot % 2 else keep_ref
            for far in range(sample):
                place = (slot ^ me) * sample + (far ^ my)
                at = (slot // 2 * sample + far) * own
                ref[at : at + own, :] = turned[pl.ds(pl.multiple_of(place * own, own), own), :]
        u = acc_u[...].reshape(times, width)
        three = three_ref[...].astype(F32)
        tail = space // 2 * sample * own
        third = u * four_ref[...].astype(F32)
        fourth = jnp.sum(u * three, axis=0, keepdims=True)
        fourth = jnp.concatenate([fourth, jnp.zeros((7, width), F32)], axis=0)
        for ref in (keep_ref, send_ref):
            ref[tail : tail + times, :] = third
            ref[tail + times :, :] = fourth
        narrow, rows = width // sample, points // sample
        for far in range(sample):
            piece = jnp.zeros((points, narrow), F32)
            for s in range(sample):
                piece = jnp.where((far ^ my) == s, acc_one[:, s * narrow : (s + 1) * narrow], piece)
            first_ref[far] = jnp.concatenate(
                [piece[n * rows : (n + 1) * rows] for n in range(sample)], axis=1
            )


def sketch_partial(ensemble, map_one, map_two, map_three, map_four, space, sample, block):
    times, _, points, cols = ensemble.shape
    width = map_two.shape[1]
    own = cols // (space * sample)
    shape = jax.ShapeDtypeStruct((space // 2 * sample * own + times + 8, width), F32)
    first = jax.ShapeDtypeStruct((sample, points // sample, width), F32)
    whole = lambda i: (0, 0)
    full = lambda a: pl.BlockSpec(a.shape, whole)
    return pl.pallas_call(
        functools.partial(sketch_kernel, space, sample, block),
        grid=(times // block,),
        in_specs=[
            pl.BlockSpec((block, 1, points, cols), lambda i: (i, 0, 0, 0)),
            full(map_one), full(map_two), full(map_three), full(map_four),
        ],
        out_specs=[full(shape), full(shape), pl.BlockSpec(first.shape, lambda i: (0, 0, 0))],
        out_shape=[shape, shape, first],
        scratch_shapes=[
            pltpu.VMEM((points, width), F32),
            pltpu.VMEM((width, cols), F32),
            pltpu.VMEM((times // block, block, width), F32),
            pltpu.VMEM((times // block, block, width), F32),
            pltpu.VMEM((times // block, width, 128), F32),
            pltpu.VMEM((width, points), F32),
            pltpu.VMEM((cols, width), F32),
        ],
        compiler_params=pltpu.CompilerParams(vmem_limit_bytes=32 * MIB),
        cost_estimate=pl.CostEstimate(
            flops=4 * ensemble.size * width, bytes_accessed=2 * ensemble.size, transcendentals=0
        ),
        name="sketch_partial",
    )(ensemble, map_one, map_two, map_three, map_four)


def final_kernel(own, *refs):
    *parts, three_ref, four_ref, out_ref, left_ref, base_ref = refs
    sample = len(parts)
    step = pl.program_id(0)
    times, rank = three_ref.shape
    wide = rank // sample

    @pl.when(step == 0)
    def _():
        my = lax.axis_index("sample")
        three = three_ref[...].astype(F32)
        three = jnp.concatenate([three, jnp.zeros((rank - times, rank), F32)], axis=0).T
        three = three[:, :times].astype(BF16)
        three = jnp.concatenate([three, three], axis=1)
        held = [part[...] for part in parts]
        for b in range(own):
            for g in range(sample):
                lanes = [
                    h[b * times : (b + 1) * times, g * wide : (g + 1) * wide] for h in held
                ]
                high, low = split(jnp.concatenate(lanes, axis=1))
                both = jnp.concatenate([high, low], axis=0)
                high, low = split(jnp.dot(three, both, preferred_element_type=F32))
                left_ref[b, g] = jnp.concatenate([high, low], axis=1)
        four = four_ref[...].astype(F32)
        which = lax.broadcasted_iota(jnp.int32, (sample, rank), 0)
        odd = lax.broadcasted_iota(jnp.int32, (wide, 2 * rank), 0) % 2
        side = lax.broadcasted_iota(jnp.int32, (wide, 2 * rank), 1) // rank
        pieces = []
        for r in range(sample):
            line = jnp.sum(jnp.where(which == (r ^ my), four, 0.0), axis=0, keepdims=True)
            line = jnp.concatenate([line, line], axis=1)
            pieces.append(jnp.where(odd == side, line, 0.0))
        base_ref[...] = jnp.concatenate(pieces * 2, axis=0)

    row = lax.broadcasted_iota(jnp.int32, base_ref.shape, 0)
    right = jnp.where((row % wide) // 2 == step, base_ref[...], 0.0).astype(BF16)
    for b in range(own):
        left = left_ref[b].reshape(sample * rank, 2 * rank)
        out = jnp.dot(left, right, preferred_element_type=F32)
        for g in range(sample):
            for side in range(2):
                out_ref[2 * g + side, b * rank : (b + 1) * rank, :] = out[
                    g * rank : (g + 1) * rank, side * rank : (side + 1) * rank
                ]


def final_core(parts, core_three, core_four):
    sample = len(parts)
    times, rank = core_three.shape
    own = parts[0].shape[0] // times
    whole = lambda i: (0, 0)
    full = lambda a: pl.BlockSpec(a.shape, whole)
    out = jax.ShapeDtypeStruct((rank, own * rank, rank), F32)
    return pl.pallas_call(
        functools.partial(final_kernel, own),
        grid=(rank // (2 * sample),),
        in_specs=[full(a) for a in parts] + [full(core_three), full(core_four)],
        out_specs=pl.BlockSpec((2 * sample, own * rank, rank), lambda i: (i, 0, 0)),
        out_shape=out,
        scratch_shapes=[
            pltpu.VMEM((own, sample, rank, 2 * rank), BF16),
            pltpu.VMEM((2 * rank, 2 * rank), F32),
        ],
        compiler_params=pltpu.CompilerParams(vmem_limit_bytes=24 * MIB),
        cost_estimate=pl.CostEstimate(
            flops=2 * out.size * 2 * rank, bytes_accessed=4 * out.size, transcendentals=0
        ),
        name="final_core",
    )(*parts, core_three, core_four)


def swap(value, axis, mask):
    size = lax.axis_size(axis)
    return lax.ppermute(value, axis, [(i, i ^ mask) for i in range(size)])


def reduce_chips(pieces, order):
    for bit in order:
        go = [u for u in pieces if u & bit]
        got = swap(jnp.concatenate([pieces[u] for u in go], axis=0), "space", 2 * bit)
        rows = got.shape[0] // len(go)
        pieces = {
            u ^ bit: pieces[u ^ bit] + got[n * rows : (n + 1) * rows] for n, u in enumerate(go)
        }
    return pieces[0]


def send_core(keep, send, space, sample):
    chips = space // 2
    bits = [1 << n for n in range(chips.bit_length() - 1)]
    summed = keep + swap(send, "space", 1)
    rows = summed.shape[0] // chips
    ways = max(1, min(2, len(bits)))
    parts = []
    size = rows // ways
    for way in range(ways):
        pieces = {
            u: summed[u * rows + way * size : u * rows + (way + 1) * size] for u in range(chips)
        }
        parts.append(reduce_chips(pieces, bits[way:] + bits[:way]))
    own = rows // sample
    got = []
    for far in range(sample):
        at = far * own
        piece = parts[at // size][at % size : at % size + own]
        got.append(swap(piece, "sample", far) if far else piece)
    return got


def add_kernel(count, rows, tail, *refs):
    keep_ref, got_ref, *outs = refs
    end = keep_ref[count * rows :, :] + got_ref[count * rows :, :]
    for u in range(count):
        at = slice(u * rows, (u + 1) * rows)
        outs[u][:rows, :] = keep_ref[at, :] + got_ref[at, :]
        outs[u][rows:, :] = end


def mix_kernel(sample, own, times, count, *refs):
    ins, first_ref, outs, fourth_ref = refs[:count], refs[count], refs[count + 1 : -1], refs[-1]
    total = ins[0][...]
    for ref in ins[1:]:
        total = total + ref[...]
    tail = sample * own
    third = total[tail : tail + times]
    for far in range(sample):
        outs[far][:own, :] = total[far * own : (far + 1) * own]
        outs[far][own : own + times, :] = third
        outs[far][own + times :, :] = first_ref[far]
    fourth_ref[...] = total[tail + times : tail + times + 1]


def end_kernel(sample, own, times, *refs):
    ins, (one_ref, two_ref, three_ref) = refs[:sample], refs[sample:]
    total = ins[0][...]
    for ref in ins[1:]:
        total = total + ref[...]
    two_ref[...] = total[:own]
    three_ref[...] = total[own : own + times]
    narrow, rows = one_ref.shape[1], one_ref.shape[0] // sample
    for n in range(sample):
        one_ref[n * rows : (n + 1) * rows, :] = total[
            own + times :, n * narrow : (n + 1) * narrow
        ]


def small_call(kernel, outs, name, *args):
    return pl.pallas_call(
        kernel,
        out_shape=[jax.ShapeDtypeStruct(s, F32) for s in outs],
        compiler_params=pltpu.CompilerParams(vmem_limit_bytes=16 * MIB),
        cost_estimate=pl.CostEstimate(
            flops=sum(a.size for a in args),
            bytes_accessed=4 * sum(a.size for a in args),
            transcendentals=0,
        ),
        name=name,
    )(*args)


def send_sketches(keep, send, first, space, sample, points, times):
    chips = space // 2
    width = keep.shape[1]
    tail = times + 8
    rows = (keep.shape[0] - tail) // chips
    own = rows // sample
    got = swap(send, "space", 1)
    pieces = small_call(
        functools.partial(add_kernel, chips, rows, tail),
        [(rows + tail, width)] * chips, "add_cores", keep, got,
    )
    pieces = [swap(p, "space", 2 * u) if u else p for u, p in enumerate(pieces)]
    length = own + times + points // sample
    *pieces, fourth = small_call(
        functools.partial(mix_kernel, sample, own, times, chips),
        [(length, width)] * sample + [(1, width)], "add_chips", *pieces, first,
    )
    pieces = [swap(p, "sample", far) if far else p for far, p in enumerate(pieces)]
    one, two, three = small_call(
        functools.partial(end_kernel, sample, own, times),
        [(points, width // sample), (own, width), (times, width)], "add_samples", *pieces,
    )
    return one, two, three, fourth


def on_device(
    ensemble, map_one, map_two, map_three, map_four, core_one, core_two, core_three, core_four
):
    space, sample = lax.axis_size("space"), lax.axis_size("sample")
    times, _, points, _ = ensemble.shape
    keep, send = core_partial(ensemble, core_one, core_two, space, sample, 8)
    parts = send_core(keep, send, space, sample)
    keep, send, first = sketch_partial(
        ensemble, map_one, map_two, map_three, map_four, space, sample, 8
    )
    one, two, three, fourth = send_sketches(keep, send, first, space, sample, points, times)
    core = final_core(parts, core_three, core_four)
    return (one, two, three, fourth, core)


def solution(mesh):
    placed = (
        P(None, "sample", "space", None),
        P("space", None),
        P(),
        P(),
        P("sample", None),
        P(),
        P(),
        P(),
        P(),
    )
    return jax.shard_map(
        on_device,
        mesh=mesh,
        in_specs=placed,
        out_specs=(
            P("space", "sample"),
            P(("space", "sample"), None),
            P(),
            P("sample", None),
            P(None, ("space", "sample"), None),
        ),
        check_vma=False,
    )
```

```python
import functools

import jax
import jax.numpy as jnp
from jax import lax
from jax.experimental import pallas as pl
from jax.experimental.pallas import tpu as pltpu
from jax.sharding import PartitionSpec as P

BF16 = jnp.bfloat16
F32 = jnp.float32
NT = (((1,), (1,)), ((), ()))
MIB = 1 << 20
CHUNKS = 1
SPAN, SLOTS = 4, 4
LIGHT = pl.CostEstimate(flops=1, bytes_accessed=1, transcendentals=0)


def split(value):
    high = value.astype(BF16)
    return high, (value - high.astype(F32)).astype(BF16)


def core_kernel(
    space, sample, block, chunks, x_hbm, two_hbm, one_hbm, *refs
):
    outs, (x_ref, two_ref, one_ref, left_ref, right_ref, sems) = refs[: 2 * chunks], refs[2 * chunks :]
    times, points, _ = x_ref.shape
    rank = two_ref.shape[1]
    half = rank // 2
    count = times // block
    me, my = lax.axis_index("space"), lax.axis_index("sample")
    copies = [
        pltpu.make_async_copy(two_hbm, two_ref, sems.at[count]),
        pltpu.make_async_copy(
            one_hbm.at[pl.ds(pl.multiple_of(me * points, points), points)], one_ref, sems.at[count + 1]
        ),
    ]
    loads = [
        pltpu.make_async_copy(
            x_hbm.at[pl.ds(n * block, block), 0], x_ref.at[pl.ds(n * block, block)], sems.at[n]
        )
        for n in range(count)
    ]
    for copy in copies + loads:
        copy.start()
    own = rank // (space * sample)
    piece = own // chunks
    slot = lax.broadcasted_iota(jnp.int32, (rank, rank), 0)
    column = lax.broadcasted_iota(jnp.int32, (rank, rank), 1)
    odd = slot // half
    rest = slot % half
    part = rest // (half // chunks)
    rest = rest % (half // chunks)
    inner = rest % piece
    far = (rest // piece) % sample
    chip = rest // (piece * sample)
    place = ((chip * 2 + odd) ^ me) * sample + (far ^ my)
    pick = jnp.where(column == place * own + part * piece + inner, 1.0, 0.0).astype(BF16)
    groups = sample
    wide = rank // groups
    row = lax.broadcasted_iota(jnp.int32, (rank, rank), 0)
    group, within = column // wide, column % wide
    source = (within // 2) * (2 * groups) + 2 * group + within % 2
    order = jnp.where(row == source, 1.0, 0.0).astype(BF16)
    for copy in copies:
        copy.wait()
    left_ref[...] = lax.dot_general(
        pick, two_ref[...], NT, preferred_element_type=F32
    ).astype(BF16)
    ordered = jnp.dot(one_ref[...], order, preferred_element_type=F32).astype(BF16)
    right_ref[...] = jnp.concatenate([ordered, ordered], axis=0)

    for n in range(count):
        loads[n].wait()
        x = x_ref[n * block : (n + 1) * block].reshape(block * points, x_ref.shape[2])
        first = lax.dot_general(left_ref[...], x, NT, preferred_element_type=F32)
        rows = []
        for t in range(block):
            high, low = split(first[:, t * points : (t + 1) * points])
            rows.append(jnp.concatenate([high, low], axis=1))
        out = jnp.dot(
            jnp.concatenate(rows, axis=0), right_ref[...], preferred_element_type=F32
        )
        size = half // chunks
        for t in range(block):
            for k in range(2 * chunks):
                at = t * rank + k * size
                outs[k][pl.ds(n * block + t, size, stride=times), :] = out[at : at + size]


def core_partial(ensemble, core_one, core_two, space, sample, block, chunks):
    times, _, points, width = ensemble.shape
    rank = core_two.shape[1]
    shape = jax.ShapeDtypeStruct((rank // 2 // chunks * times, rank), F32)
    hbm = pl.BlockSpec(memory_space=pltpu.HBM)
    return pl.pallas_call(
        functools.partial(core_kernel, space, sample, block, chunks),
        in_specs=[hbm] * 3,
        out_specs=[pl.BlockSpec(memory_space=pltpu.VMEM)] * (2 * chunks),
        out_shape=[shape] * (2 * chunks),
        scratch_shapes=[
            pltpu.VMEM((times, points, width), BF16),
            pltpu.VMEM(core_two.shape, BF16),
            pltpu.VMEM((points, rank), BF16),
            pltpu.VMEM((rank, width), BF16),
            pltpu.VMEM((2 * points, rank), BF16),
            pltpu.SemaphoreType.DMA((times // block + 2,)),
        ],
        compiler_params=pltpu.CompilerParams(vmem_limit_bytes=28 * MIB),
        cost_estimate=LIGHT,
        name="core_partial",
    )(
        pltpu.with_memory_space_constraint(ensemble, pltpu.HBM),
        pltpu.with_memory_space_constraint(core_two, pltpu.HBM),
        pltpu.with_memory_space_constraint(core_one, pltpu.HBM),
    )


def sketch_kernel(
    space, sample, block, x_hbm, one_ref, two_ref, three_ref, four_ref, after_ref,
    keep_ref, send_ref, first_ref,
    x_ref, acc_one, acc_two, acc_u, pairs, rolled, one_t, turned, sems,
):
    del after_ref
    times, points, cols = x_ref.shape
    width = two_ref.shape[1]
    count = times // block
    loads = [
        pltpu.make_async_copy(
            x_hbm.at[pl.ds(n * block, block), 0], x_ref.at[pl.ds(n * block, block)], sems.at[n]
        )
        for n in range(count)
    ]
    for load in loads:
        load.start()
    acc_one[...] = jnp.zeros_like(acc_one)
    acc_two[...] = jnp.zeros_like(acc_two)
    four = four_ref[...].astype(F32)
    pair = three_ref[...].astype(F32) * four
    pairs[...] = pair.reshape(pairs.shape)
    padded = jnp.concatenate([pair, jnp.zeros((128 - times, width), F32)], axis=0)
    flipped = padded.T
    for n in range(count):
        rolled[n] = pltpu.roll(flipped, (128 - n * block) % 128, 1)
    one = one_ref[...].astype(F32)
    if points < 128:
        one = jnp.concatenate([one, jnp.zeros((128 - points, width), F32)], axis=0)
    one_t[...] = one.T[:, :points]

    for step in range(count):
        loads[step].wait()
        x = x_ref[step * block : (step + 1) * block].reshape(block * points, cols)
        proj = jnp.dot(x, two_ref[...], preferred_element_type=F32)
        one = one_ref[...].astype(F32)
        weights = rolled[step]
        total = acc_one[...]
        sums, krao = [], []
        for t in range(block):
            part = proj[t * points : (t + 1) * points]
            total = total + part * pairs[step, t : t + 1, :]
            sums.append(jnp.sum(part * one, axis=0, keepdims=True))
            krao.append((weights[:, t : t + 1] * one_t[...]).astype(BF16))
        acc_one[...] = total
        acc_u[step] = jnp.concatenate(sums, axis=0)
        acc_two[...] += jnp.dot(
            jnp.concatenate(krao, axis=1), x, preferred_element_type=F32
        )

    me, my = lax.axis_index("space"), lax.axis_index("sample")
    turned[...] = acc_two[...].T
    own = cols // (space * sample)
    for slot in range(space):
        ref = send_ref if slot % 2 else keep_ref
        for far in range(sample):
            place = (slot ^ me) * sample + (far ^ my)
            at = (slot // 2 * sample + far) * own
            ref[at : at + own, :] = turned[pl.ds(pl.multiple_of(place * own, own), own), :]
    u = acc_u[...].reshape(times, width)
    three = three_ref[...].astype(F32)
    tail = space // 2 * sample * own
    third = u * four_ref[...].astype(F32)
    fourth = jnp.sum(u * three, axis=0, keepdims=True)
    fourth = jnp.concatenate([fourth, jnp.zeros((7, width), F32)], axis=0)
    for ref in (keep_ref, send_ref):
        ref[tail : tail + times, :] = third
        ref[tail + times :, :] = fourth
    narrow, folds = width // sample, width // points
    lines = narrow // folds
    square = acc_one[...]
    if points < 128:
        square = jnp.concatenate([square, jnp.zeros((128 - points, width), F32)], axis=0)
    turned[:width, :128] = square.T
    for far in range(sample):
        at = (far ^ my) * narrow
        pieces = [
            turned[pl.ds(pl.multiple_of(at + n * lines, 8), lines), :points] for n in range(folds)
        ]
        first_ref[far] = jnp.concatenate(pieces, axis=1)


def sketch_partial(
    ensemble, map_one, map_two, map_three, map_four, after, space, sample, block
):
    times, _, points, cols = ensemble.shape
    width = map_two.shape[1]
    own = cols // (space * sample)
    shape = jax.ShapeDtypeStruct((space // 2 * sample * own + times + 8, width), F32)
    first = jax.ShapeDtypeStruct((sample, points // sample, width), F32)
    anywhere = pl.BlockSpec(memory_space=pl.ANY)
    return pl.pallas_call(
        functools.partial(sketch_kernel, space, sample, block),
        in_specs=[pl.BlockSpec(memory_space=pltpu.HBM)]
        + [pl.BlockSpec(memory_space=pltpu.VMEM)] * 4
        + [anywhere],
        out_specs=[pl.BlockSpec(memory_space=pltpu.VMEM)] * 3,
        out_shape=[shape, shape, first],
        scratch_shapes=[
            pltpu.VMEM((times, points, cols), BF16),
            pltpu.VMEM((points, width), F32),
            pltpu.VMEM((width, cols), F32),
            pltpu.VMEM((times // block, block, width), F32),
            pltpu.VMEM((times // block, block, width), F32),
            pltpu.VMEM((times // block, width, 128), F32),
            pltpu.VMEM((width, points), F32),
            pltpu.VMEM((cols, width), F32),
            pltpu.SemaphoreType.DMA((times // block,)),
        ],
        compiler_params=pltpu.CompilerParams(vmem_limit_bytes=32 * MIB),
        cost_estimate=LIGHT,
        name="sketch_partial",
    )(
        pltpu.with_memory_space_constraint(ensemble, pltpu.HBM),
        map_one, map_two, map_three, map_four, after,
    )


def final_kernel(sample, place, *refs):
    start, first, count, _ = place
    *ins, out_hbm, token_ref, left_ref, base_ref, ring, sems = refs
    parts, (three_ref, four_ref) = ins[:sample], ins[sample : sample + 2]
    times, rank = three_ref.shape
    wide = rank // sample
    slots, each = ring.shape[0], ring.shape[1]
    span = each // (2 * sample)
    my = lax.axis_index("sample")

    token_ref[...] = jnp.zeros_like(token_ref)
    three = three_ref[...].astype(F32)
    three = jnp.concatenate([three, jnp.zeros((rank - times, rank), F32)], axis=0).T
    three = three[:, :times].astype(BF16)
    three = jnp.concatenate([three, three], axis=1)
    four = four_ref[...].astype(F32)
    which = lax.broadcasted_iota(jnp.int32, (sample, rank), 0)
    odd = lax.broadcasted_iota(jnp.int32, (wide, 2 * rank), 0) % 2
    side = lax.broadcasted_iota(jnp.int32, (wide, 2 * rank), 1) // rank
    pieces = []
    for r in range(sample):
        line = jnp.sum(jnp.where(which == (r ^ my), four, 0.0), axis=0, keepdims=True)
        line = jnp.concatenate([line, line], axis=1)
        pieces.append(jnp.where(odd == side, line, 0.0))
    base_ref[...] = jnp.concatenate(pieces * 2, axis=0)
    row = (lax.broadcasted_iota(jnp.int32, base_ref.shape, 0) % wide) // 2

    def copy(b, slot, group):
        at = pl.multiple_of((first + b) * rank, rank)
        return pltpu.make_async_copy(
            ring.at[slot],
            out_hbm.at[pl.ds(group * each, each), pl.ds(at, rank)],
            sems.at[slot],
        )

    groups = rank // each

    def block(b):
        held = [
            part[pl.ds(pl.multiple_of((start + b) * times, 8), times), :] for part in parts
        ]
        joined = []
        for g in range(sample):
            joined += [h[:, g * wide : (g + 1) * wide] for h in held]
        high, low = split(jnp.concatenate(joined, axis=1))
        both = jnp.concatenate([high, low], axis=0)
        high, low = split(jnp.dot(three, both, preferred_element_type=F32))
        for g in range(sample):
            at = slice(g * rank, (g + 1) * rank)
            left_ref[at, :] = jnp.concatenate([high[:, at], low[:, at]], axis=1)

        def some(n, _):
            for slot in range(slots):
                group = n * slots + slot

                @pl.when((b > 0) | (n > 0))
                def _():
                    copy(0, slot, 0).wait()

                for m in range(span):
                    right = jnp.where(row == group * span + m, base_ref[...], 0.0).astype(BF16)
                    out = jnp.dot(left_ref[...], right, preferred_element_type=F32)
                    for g in range(sample):
                        for k in range(2):
                            ring[slot, m * 2 * sample + 2 * g + k] = out[
                                g * rank : (g + 1) * rank, k * rank : (k + 1) * rank
                            ]
                copy(b, slot, group).start()

        lax.fori_loop(0, groups // slots, some, None)

    pl.loop(0, count)(block)
    for slot in range(slots):
        copy(0, slot, 0).wait()


def final_core(parts, core_three, core_four, after, place, into):
    sample = len(parts)
    rank = core_three.shape[1]
    vmem, anywhere = pl.BlockSpec(memory_space=pltpu.VMEM), pl.BlockSpec(memory_space=pl.ANY)
    extra = list(after) + ([into] if into is not None else [])
    each = min(rank, 2 * sample * SPAN)
    slots = min(SLOTS, rank // each)
    return pl.pallas_call(
        functools.partial(final_kernel, sample, place),
        in_specs=[vmem] * (sample + 2) + [anywhere] * len(extra),
        out_specs=[anywhere, vmem],
        out_shape=[
            jax.ShapeDtypeStruct((rank, place[3] * rank, rank), F32),
            jax.ShapeDtypeStruct((8, 128), F32),
        ],
        scratch_shapes=[
            pltpu.VMEM((sample * rank, 2 * rank), BF16),
            pltpu.VMEM((2 * rank, 2 * rank), F32),
            pltpu.VMEM((slots, each, rank, rank), F32),
            pltpu.SemaphoreType.DMA((slots,)),
        ],
        input_output_aliases={sample + 1 + len(extra): 0} if into is not None else {},
        compiler_params=pltpu.CompilerParams(vmem_limit_bytes=32 * MIB),
        cost_estimate=LIGHT,
        name="final_core",
    )(*parts, core_three, core_four, *extra)


def swap(value, axis, mask):
    size = lax.axis_size(axis)
    return lax.ppermute(value, axis, [(i, i ^ mask) for i in range(size)])


def small_call(kernel, outs, name, args, after=()):
    vmem, anywhere = pl.BlockSpec(memory_space=pltpu.VMEM), pl.BlockSpec(memory_space=pl.ANY)
    count = len(args)

    def body(*refs):
        kernel(*refs[:count], *refs[count + len(after) :])

    return pl.pallas_call(
        body,
        in_specs=[vmem] * count + [anywhere] * len(after),
        out_specs=[vmem] * len(outs),
        out_shape=[jax.ShapeDtypeStruct(s, F32) for s in outs],
        compiler_params=pltpu.CompilerParams(vmem_limit_bytes=16 * MIB),
        cost_estimate=LIGHT,
        name=name,
    )(*args, *after)


def route(blocks, bit):
    stay = [u for u in blocks if not u & bit]
    return [u ^ bit for u in stay], stay


def core_kernel_add(rows, first, plans, *refs):
    ways = len(plans)
    ins, outs = refs[: 2 if first else 2 * ways], list(refs[2 if first else 2 * ways :])
    for way, (slots, bit) in enumerate(plans):
        stay, came = ins if first else ins[2 * way : 2 * way + 2]

        def total(n):
            u = slots[n]
            at = slice((u * ways + way) * rows, (u * ways + way + 1) * rows)
            if not first:
                at = slice(n * rows, (n + 1) * rows)
            return stay[at, :] + came[at, :]

        if bit:
            for chosen in route(slots, bit):
                out = outs.pop(0)
                for n, u in enumerate(chosen):
                    out[n * rows : (n + 1) * rows, :] = total(slots.index(u))
        else:
            value = total(0)
            each = outs[0].shape[0]
            for n in range(rows // each):
                outs.pop(0)[...] = value[n * each : (n + 1) * each]


def core_stage(values, plans, rows, first, sample, rank, after):
    ways = len(plans)
    shapes = []
    for slots, bit in plans:
        if bit:
            shapes += [(len(slots) // 2 * rows, rank)] * 2
        else:
            shapes += [(rows // (sample // ways), rank)] * (sample // ways)
    return small_call(
        functools.partial(core_kernel_add, rows, first, plans), shapes, "add_core", values, after
    )


def core_tree(space, sample):
    chips = space // 2
    bits = [1 << n for n in range(chips.bit_length() - 1)]
    ways = 2 if len(bits) > 1 and sample % 2 == 0 else 1
    orders = [bits[way:] + bits[:way] for way in range(ways)]
    held = [list(range(chips)) for _ in range(ways)]
    stages = []
    for n in range(len(bits) + 1):
        plans = []
        for way in range(ways):
            bit = orders[way][n] if n < len(bits) else 0
            plans.append((held[way], bit))
            if bit:
                held[way] = route(held[way], bit)[1]
        stages.append(plans)
    return stages


def add_kernel(blocks, rows, tail, *refs):
    keep_ref, got_ref, *outs = refs
    at = keep_ref.shape[0] - tail
    end = keep_ref[at:, :] + got_ref[at:, :]
    for u, out in zip(blocks, outs):
        at = slice(u * rows, (u + 1) * rows)
        out[:rows, :] = keep_ref[at, :] + got_ref[at, :]
        out[rows:, :] = end


def mix_kernel(sample, own, times, count, *refs):
    ins, first_ref, outs, fourth_ref = refs[:count], refs[count], refs[count + 1 : -1], refs[-1]
    total = ins[0][...]
    for ref in ins[1:]:
        total = total + ref[...]
    tail = sample * own
    third = total[tail : tail + times]
    for far in range(sample):
        outs[far][:own, :] = total[far * own : (far + 1) * own]
        outs[far][own : own + times, :] = third
        outs[far][own + times :, :] = first_ref[far]
    fourth_ref[...] = total[tail + times : tail + times + 1]


def end_kernel(sample, own, times, *refs):
    ins, (one_ref, two_ref, three_ref) = refs[:sample], refs[sample:]
    total = ins[0][...]
    for ref in ins[1:]:
        total = total + ref[...]
    two_ref[...] = total[:own]
    three_ref[...] = total[own : own + times]
    lines = total.shape[0] - own - times
    points = one_ref.shape[1]
    for n in range(one_ref.shape[0] // lines):
        one_ref[n * lines : (n + 1) * lines, :] = total[
            own + times :, n * points : (n + 1) * points
        ]


def on_device(
    ensemble, map_one, map_two, map_three, map_four, core_one, core_two, core_three, core_four
):
    space, sample = lax.axis_size("space"), lax.axis_size("sample")
    times, _, points, _ = ensemble.shape
    rank, width = core_two.shape[1], map_two.shape[1]
    chips = space // 2
    chunks = min(CHUNKS, rank // (space * sample))
    every = range(chunks)

    sent = core_partial(ensemble, core_one, core_two, space, sample, 8, chunks)
    keep, send = sent[:chunks], sent[chunks:]
    got = [swap(s, "space", 1) for s in send]
    stages = core_tree(space, sample)
    ways = len(stages[0])
    rows = keep[0].shape[0] // (chips * ways)
    state = [[keep[k], got[k]] for k in every]
    last = None
    for n, plans in enumerate(stages):
        for k in every:
            after = [] if last is None else [last]
            outs = core_stage(state[k], plans, rows, n == 0, sample, rank, after)
            last = outs[-1]
            if n + 1 < len(stages):
                state[k] = []
                for way, (_, bit) in enumerate(plans):
                    went, stayed = outs[2 * way : 2 * way + 2]
                    state[k] += [stayed, swap(went, "space", 2 * bit)]
            else:
                state[k] = [swap(p, "sample", far) if far else p for far, p in enumerate(outs)]
        if n == 0:
            mine, send, first = sketch_partial(
                ensemble, map_one, map_two, map_three, map_four, last, space, sample, 8
            )
            last = first
            theirs = swap(send, "space", 1)

    tail = times + 8
    lines = (mine.shape[0] - tail) // chips
    own = lines // sample
    near = [u for u in range(chips) if u & (u - 1) == 0]
    pieces = []
    for blocks, after in (
        (near, last),
        ([u for u in range(chips) if u not in near], state[-1][min(1, sample - 1)]),
    ):
        outs = small_call(
            functools.partial(add_kernel, blocks, lines, tail),
            [(lines + tail, width)] * len(blocks), "add_cores", [mine, theirs], [after],
        ) if blocks else []
        pieces += [swap(p, "space", 2 * u) if u else p for u, p in zip(blocks, outs)]

    total = rank // (space * sample)
    piece = total // chunks
    calls = [(k, 0, k * piece, piece) for k in every]
    if chunks == 1 and total > 1:
        calls = [(0, 0, 0, 1), (0, 1, 1, total - 1)]
    core, after = None, []
    for k, start, at, count in calls[:-1]:
        core, token = final_core(
            state[k], core_three, core_four, after, (start, at, count, total), core
        )
        after = [token]
    length = own + times + first.shape[1]
    *pieces, fourth = small_call(
        functools.partial(mix_kernel, sample, own, times, chips),
        [(length, width)] * sample + [(1, width)], "add_chips", [*pieces, first], after,
    )
    k, start, at, count = calls[-1]
    core, _ = final_core(
        state[k], core_three, core_four, [pieces[0]], (start, at, count, total), core
    )
    pieces = [swap(p, "sample", far) if far else p for far, p in enumerate(pieces)]
    one, two, three = small_call(
        functools.partial(end_kernel, sample, own, times),
        [(width // sample, points), (own, width), (times, width)], "add_samples", pieces,
    )
    return (one.T, two, three, fourth, core)


def solution(mesh):
    placed = (
        P(None, "sample", "space", None),
        P("space", None),
        P(),
        P(),
        P("sample", None),
        P(),
        P(),
        P(),
        P(),
    )
    return jax.shard_map(
        on_device,
        mesh=mesh,
        in_specs=placed,
        out_specs=(
            P("space", "sample"),
            P(("space", "sample"), None),
            P(),
            P("sample", None),
            P(None, ("space", "sample"), None),
        ),
        check_vma=False,
    )
```

```python
import functools

import jax
import jax.numpy as jnp
from jax import lax
from jax.experimental import pallas as pl
from jax.experimental.pallas import tpu as pltpu
from jax.sharding import PartitionSpec as P

BF16 = jnp.bfloat16
F32 = jnp.float32
NT = (((1,), (1,)), ((), ()))
MIB = 1 << 20
CHUNKS = 1
BLOCK, PORTIONS = 4, (2, 4, 6)
SPAN, SLOTS = 4, 4
LIGHT = pl.CostEstimate(flops=1, bytes_accessed=1, transcendentals=0)


def split(value):
    high = value.astype(BF16)
    return high, (value - high.astype(F32)).astype(BF16)


def portions(times, block):
    lengths = [n * block for n in PORTIONS]
    while sum(lengths) < times:
        lengths.append(min(lengths[-1], times - sum(lengths)))
    return lengths


def core_kernel(
    space, sample, block, chunks, x_hbm, two_hbm, one_hbm, *refs
):
    outs, (x_ref, two_ref, one_ref, left_ref, right_ref, sems) = refs[: 2 * chunks], refs[2 * chunks :]
    times, points, _ = x_ref.shape
    rank = two_ref.shape[1]
    half = rank // 2
    count = times // block
    me, my = lax.axis_index("space"), lax.axis_index("sample")
    copies = [
        pltpu.make_async_copy(two_hbm, two_ref, sems.at[count]),
        pltpu.make_async_copy(
            one_hbm.at[pl.ds(pl.multiple_of(me * points, points), points)], one_ref, sems.at[count + 1]
        ),
    ]
    loads = [
        pltpu.make_async_copy(
            x_hbm.at[pl.ds(n * block, block), 0], x_ref.at[pl.ds(n * block, block)], sems.at[n]
        )
        for n in range(count)
    ]
    for copy in copies + loads:
        copy.start()
    own = rank // (space * sample)
    piece = own // chunks
    slot = lax.broadcasted_iota(jnp.int32, (rank, rank), 0)
    column = lax.broadcasted_iota(jnp.int32, (rank, rank), 1)
    odd = slot // half
    rest = slot % half
    part = rest // (half // chunks)
    rest = rest % (half // chunks)
    inner = rest % piece
    far = (rest // piece) % sample
    chip = rest // (piece * sample)
    place = ((chip * 2 + odd) ^ me) * sample + (far ^ my)
    pick = jnp.where(column == place * own + part * piece + inner, 1.0, 0.0).astype(BF16)
    groups = sample
    wide = rank // groups
    row = lax.broadcasted_iota(jnp.int32, (rank, rank), 0)
    group, within = column // wide, column % wide
    source = (within // 2) * (2 * groups) + 2 * group + within % 2
    order = jnp.where(row == source, 1.0, 0.0).astype(BF16)
    for copy in copies:
        copy.wait()
    left_ref[...] = lax.dot_general(
        pick, two_ref[...], NT, preferred_element_type=F32
    ).astype(BF16)
    ordered = jnp.dot(one_ref[...], order, preferred_element_type=F32).astype(BF16)
    right_ref[...] = jnp.concatenate([ordered, ordered], axis=0)

    size = half // chunks
    start = 0
    for length in portions(times, block):
        for n in range(start // block, (start + length) // block):
            loads[n].wait()
        x = x_ref[start : start + length].reshape(length * points, x_ref.shape[2])
        first = lax.dot_general(left_ref[...], x, NT, preferred_element_type=F32)
        rows = []
        for t in range(length):
            high, low = split(first[:, t * points : (t + 1) * points])
            rows.append(jnp.concatenate([high, low], axis=1))
        out = jnp.dot(
            jnp.concatenate(rows, axis=0), right_ref[...], preferred_element_type=F32
        )
        for t in range(length):
            for k in range(2 * chunks):
                at = t * rank + k * size
                outs[k][pl.ds(start + t, size, stride=times), :] = out[at : at + size]
        start += length


def core_partial(ensemble, core_one, core_two, space, sample, block, chunks):
    times, _, points, width = ensemble.shape
    rank = core_two.shape[1]
    shape = jax.ShapeDtypeStruct((rank // 2 // chunks * times, rank), F32)
    hbm = pl.BlockSpec(memory_space=pltpu.HBM)
    return pl.pallas_call(
        functools.partial(core_kernel, space, sample, block, chunks),
        in_specs=[hbm] * 3,
        out_specs=[pl.BlockSpec(memory_space=pltpu.VMEM)] * (2 * chunks),
        out_shape=[shape] * (2 * chunks),
        scratch_shapes=[
            pltpu.VMEM((times, points, width), BF16),
            pltpu.VMEM(core_two.shape, BF16),
            pltpu.VMEM((points, rank), BF16),
            pltpu.VMEM((rank, width), BF16),
            pltpu.VMEM((2 * points, rank), BF16),
            pltpu.SemaphoreType.DMA((times // block + 2,)),
        ],
        compiler_params=pltpu.CompilerParams(vmem_limit_bytes=28 * MIB),
        cost_estimate=LIGHT,
        name="core_partial",
    )(
        pltpu.with_memory_space_constraint(ensemble, pltpu.HBM),
        pltpu.with_memory_space_constraint(core_two, pltpu.HBM),
        pltpu.with_memory_space_constraint(core_one, pltpu.HBM),
    )


def sketch_kernel(
    space, sample, block, x_hbm, one_ref, two_ref, three_ref, four_ref, after_ref,
    keep_ref, send_ref, first_ref,
    x_ref, acc_one, acc_two, acc_u, pairs, flipped, one_t, turned, sems,
):
    del after_ref
    times, points, cols = x_ref.shape
    width = two_ref.shape[1]
    count = times // block
    loads = [
        pltpu.make_async_copy(
            x_hbm.at[pl.ds(n * block, block), 0], x_ref.at[pl.ds(n * block, block)], sems.at[n]
        )
        for n in range(count)
    ]
    for load in loads:
        load.start()
    four = four_ref[...].astype(F32)
    pair = three_ref[...].astype(F32) * four
    pairs[...] = pair
    padded = jnp.concatenate([pair, jnp.zeros((128 - times, width), F32)], axis=0)
    flipped[...] = padded.T
    one = one_ref[...].astype(F32)
    if points < 128:
        one = jnp.concatenate([one, jnp.zeros((128 - points, width), F32)], axis=0)
    one_t[...] = one.T[:, :points]

    start = 0
    for length in portions(times, block):
        for n in range(start // block, (start + length) // block):
            loads[n].wait()
        x = x_ref[start : start + length].reshape(length * points, cols)
        proj = jnp.dot(x, two_ref[...], preferred_element_type=F32)
        one = one_ref[...].astype(F32)
        total = acc_one[...] if start else jnp.zeros_like(acc_one)
        krao = []
        for t in range(length):
            at = start + t
            part = proj[t * points : (t + 1) * points]
            total = total + part * pairs[at : at + 1, :]
            acc_u[at : at + 1, :] = jnp.sum(part * one, axis=0, keepdims=True)
            krao.append((flipped[:, at : at + 1] * one_t[...]).astype(BF16))
        acc_one[...] = total
        more = jnp.dot(jnp.concatenate(krao, axis=1), x, preferred_element_type=F32)
        acc_two[...] = acc_two[...] + more if start else more
        start += length

    me, my = lax.axis_index("space"), lax.axis_index("sample")
    turned[...] = acc_two[...].T
    own = cols // (space * sample)
    for slot in range(space):
        ref = send_ref if slot % 2 else keep_ref
        for far in range(sample):
            place = (slot ^ me) * sample + (far ^ my)
            at = (slot // 2 * sample + far) * own
            ref[at : at + own, :] = turned[pl.ds(pl.multiple_of(place * own, own), own), :]
    u = acc_u[...]
    three = three_ref[...].astype(F32)
    tail = space // 2 * sample * own
    third = u * four_ref[...].astype(F32)
    fourth = jnp.sum(u * three, axis=0, keepdims=True)
    fourth = jnp.concatenate([fourth, jnp.zeros((7, width), F32)], axis=0)
    for ref in (keep_ref, send_ref):
        ref[tail : tail + times, :] = third
        ref[tail + times :, :] = fourth
    narrow, folds = width // sample, width // points
    lines = narrow // folds
    square = acc_one[...]
    if points < 128:
        square = jnp.concatenate([square, jnp.zeros((128 - points, width), F32)], axis=0)
    turned[:width, :128] = square.T
    for far in range(sample):
        at = (far ^ my) * narrow
        pieces = [
            turned[pl.ds(pl.multiple_of(at + n * lines, 8), lines), :points] for n in range(folds)
        ]
        first_ref[far] = jnp.concatenate(pieces, axis=1)


def sketch_partial(
    ensemble, map_one, map_two, map_three, map_four, after, space, sample, block
):
    times, _, points, cols = ensemble.shape
    width = map_two.shape[1]
    own = cols // (space * sample)
    shape = jax.ShapeDtypeStruct((space // 2 * sample * own + times + 8, width), F32)
    first = jax.ShapeDtypeStruct((sample, points // sample, width), F32)
    anywhere = pl.BlockSpec(memory_space=pl.ANY)
    return pl.pallas_call(
        functools.partial(sketch_kernel, space, sample, block),
        in_specs=[pl.BlockSpec(memory_space=pltpu.HBM)]
        + [pl.BlockSpec(memory_space=pltpu.VMEM)] * 4
        + [anywhere],
        out_specs=[pl.BlockSpec(memory_space=pltpu.VMEM)] * 3,
        out_shape=[shape, shape, first],
        scratch_shapes=[
            pltpu.VMEM((times, points, cols), BF16),
            pltpu.VMEM((points, width), F32),
            pltpu.VMEM((width, cols), F32),
            pltpu.VMEM((times, width), F32),
            pltpu.VMEM((times, width), F32),
            pltpu.VMEM((width, 128), F32),
            pltpu.VMEM((width, points), F32),
            pltpu.VMEM((cols, width), F32),
            pltpu.SemaphoreType.DMA((times // block,)),
        ],
        compiler_params=pltpu.CompilerParams(vmem_limit_bytes=32 * MIB),
        cost_estimate=LIGHT,
        name="sketch_partial",
    )(
        pltpu.with_memory_space_constraint(ensemble, pltpu.HBM),
        map_one, map_two, map_three, map_four, after,
    )


def final_kernel(sample, place, *refs):
    start, first, count, _ = place
    *ins, out_hbm, token_ref, left_ref, base_ref, ring, sems = refs
    parts, (three_ref, four_ref) = ins[:sample], ins[sample : sample + 2]
    times, rank = three_ref.shape
    wide = rank // sample
    slots, each = ring.shape[0], ring.shape[1]
    span = each // (2 * sample)
    my = lax.axis_index("sample")

    token_ref[...] = jnp.zeros_like(token_ref)
    three = three_ref[...].astype(F32)
    three = jnp.concatenate([three, jnp.zeros((rank - times, rank), F32)], axis=0).T
    three = three[:, :times].astype(BF16)
    three = jnp.concatenate([three, three], axis=1)
    four = four_ref[...].astype(F32)
    which = lax.broadcasted_iota(jnp.int32, (sample, rank), 0)
    odd = lax.broadcasted_iota(jnp.int32, (wide, 2 * rank), 0) % 2
    side = lax.broadcasted_iota(jnp.int32, (wide, 2 * rank), 1) // rank
    pieces = []
    for r in range(sample):
        line = jnp.sum(jnp.where(which == (r ^ my), four, 0.0), axis=0, keepdims=True)
        line = jnp.concatenate([line, line], axis=1)
        pieces.append(jnp.where(odd == side, line, 0.0))
    base_ref[...] = jnp.concatenate(pieces * 2, axis=0)
    row = (lax.broadcasted_iota(jnp.int32, base_ref.shape, 0) % wide) // 2

    def copy(b, slot, group):
        at = pl.multiple_of((first + b) * rank, rank)
        return pltpu.make_async_copy(
            ring.at[slot],
            out_hbm.at[pl.ds(group * each, each), pl.ds(at, rank)],
            sems.at[slot],
        )

    groups = rank // each

    def block(b):
        held = [
            part[pl.ds(pl.multiple_of((start + b) * times, 8), times), :] for part in parts
        ]
        joined = []
        for g in range(sample):
            joined += [h[:, g * wide : (g + 1) * wide] for h in held]
        high, low = split(jnp.concatenate(joined, axis=1))
        both = jnp.concatenate([high, low], axis=0)
        high, low = split(jnp.dot(three, both, preferred_element_type=F32))
        for g in range(sample):
            at = slice(g * rank, (g + 1) * rank)
            left_ref[at, :] = jnp.concatenate([high[:, at], low[:, at]], axis=1)

        def some(n, _):
            for slot in range(slots):
                group = n * slots + slot

                @pl.when((b > 0) | (n > 0))
                def _():
                    copy(0, slot, 0).wait()

                for m in range(span):
                    right = jnp.where(row == group * span + m, base_ref[...], 0.0).astype(BF16)
                    out = jnp.dot(left_ref[...], right, preferred_element_type=F32)
                    for g in range(sample):
                        for k in range(2):
                            ring[slot, m * 2 * sample + 2 * g + k] = out[
                                g * rank : (g + 1) * rank, k * rank : (k + 1) * rank
                            ]
                copy(b, slot, group).start()

        lax.fori_loop(0, groups // slots, some, None)

    pl.loop(0, count)(block)
    for slot in range(slots):
        copy(0, slot, 0).wait()


def final_core(parts, core_three, core_four, after, place, into):
    sample = len(parts)
    rank = core_three.shape[1]
    vmem, anywhere = pl.BlockSpec(memory_space=pltpu.VMEM), pl.BlockSpec(memory_space=pl.ANY)
    extra = list(after) + ([into] if into is not None else [])
    each = min(rank, 2 * sample * SPAN)
    slots = min(SLOTS, rank // each)
    return pl.pallas_call(
        functools.partial(final_kernel, sample, place),
        in_specs=[vmem] * (sample + 2) + [anywhere] * len(extra),
        out_specs=[anywhere, vmem],
        out_shape=[
            jax.ShapeDtypeStruct((rank, place[3] * rank, rank), F32),
            jax.ShapeDtypeStruct((8, 128), F32),
        ],
        scratch_shapes=[
            pltpu.VMEM((sample * rank, 2 * rank), BF16),
            pltpu.VMEM((2 * rank, 2 * rank), F32),
            pltpu.VMEM((slots, each, rank, rank), F32),
            pltpu.SemaphoreType.DMA((slots,)),
        ],
        input_output_aliases={sample + 1 + len(extra): 0} if into is not None else {},
        compiler_params=pltpu.CompilerParams(vmem_limit_bytes=32 * MIB),
        cost_estimate=pl.CostEstimate(
            flops=4 * rank**4, bytes_accessed=4 * place[2] * rank**3, transcendentals=0
        ),
        name="final_core",
    )(*parts, core_three, core_four, *extra)


def swap(value, axis, mask):
    size = lax.axis_size(axis)
    return lax.ppermute(value, axis, [(i, i ^ mask) for i in range(size)])


def small_call(kernel, outs, name, args, after=()):
    vmem, anywhere = pl.BlockSpec(memory_space=pltpu.VMEM), pl.BlockSpec(memory_space=pl.ANY)
    count = len(args)

    def body(*refs):
        kernel(*refs[:count], *refs[count + len(after) :])

    return pl.pallas_call(
        body,
        in_specs=[vmem] * count + [anywhere] * len(after),
        out_specs=[vmem] * len(outs),
        out_shape=[jax.ShapeDtypeStruct(s, F32) for s in outs],
        compiler_params=pltpu.CompilerParams(vmem_limit_bytes=16 * MIB),
        cost_estimate=LIGHT,
        name=name,
    )(*args, *after)


def route(blocks, bit):
    stay = [u for u in blocks if not u & bit]
    return [u ^ bit for u in stay], stay


def core_kernel_add(rows, first, plans, passed, *refs):
    ways = len(plans)
    count = 2 if first else 2 * ways
    ins, outs = refs[:count], list(refs[count:])
    if passed:
        outs[-1][...] = outs[0][...]
        outs = outs[1:-1]
    for way, (slots, bit) in enumerate(plans):
        stay, came = ins if first else ins[2 * way : 2 * way + 2]

        def total(n):
            u = slots[n]
            at = slice((u * ways + way) * rows, (u * ways + way + 1) * rows)
            if not first:
                at = slice(n * rows, (n + 1) * rows)
            return stay[at, :] + came[at, :]

        if bit:
            for chosen in route(slots, bit):
                out = outs.pop(0)
                for n, u in enumerate(chosen):
                    out[n * rows : (n + 1) * rows, :] = total(slots.index(u))
        else:
            value = total(0)
            each = outs[0].shape[0]
            for n in range(rows // each):
                outs.pop(0)[...] = value[n * each : (n + 1) * each]


def core_stage(values, plans, rows, first, sample, rank, after, passed=None):
    ways = len(plans)
    shapes = []
    for slots, bit in plans:
        if bit:
            shapes += [(len(slots) // 2 * rows, rank)] * 2
        else:
            shapes += [(rows // (sample // ways), rank)] * (sample // ways)
    if passed is not None:
        values, shapes = [*values, passed], [*shapes, passed.shape]
    return small_call(
        functools.partial(core_kernel_add, rows, first, plans, passed is not None),
        shapes, "add_core", values, after,
    )


def core_tree(space, sample):
    chips = space // 2
    bits = [1 << n for n in range(chips.bit_length() - 1)]
    ways = 2 if len(bits) > 1 and sample % 2 == 0 else 1
    orders = [bits[way:] + bits[:way] for way in range(ways)]
    held = [list(range(chips)) for _ in range(ways)]
    stages = []
    for n in range(len(bits) + 1):
        plans = []
        for way in range(ways):
            bit = orders[way][n] if n < len(bits) else 0
            plans.append((held[way], bit))
            if bit:
                held[way] = route(held[way], bit)[1]
        stages.append(plans)
    return stages


def add_kernel(blocks, rows, tail, *refs):
    keep_ref, got_ref, *outs = refs
    at = keep_ref.shape[0] - tail
    end = keep_ref[at:, :] + got_ref[at:, :]
    for u, out in zip(blocks, outs):
        at = slice(u * rows, (u + 1) * rows)
        out[:rows, :] = keep_ref[at, :] + got_ref[at, :]
        out[rows:, :] = end


def mix_kernel(sample, own, times, count, *refs):
    ins, first_ref, outs, fourth_ref = refs[:count], refs[count], refs[count + 1 : -1], refs[-1]
    total = ins[0][...]
    for ref in ins[1:]:
        total = total + ref[...]
    tail = sample * own
    third = total[tail : tail + times]
    for far in range(sample):
        outs[far][:own, :] = total[far * own : (far + 1) * own]
        outs[far][own : own + times, :] = third
        outs[far][own + times :, :] = first_ref[far]
    fourth_ref[...] = total[tail + times : tail + times + 1]


def end_kernel(sample, own, times, *refs):
    ins, (one_ref, two_ref, three_ref) = refs[:sample], refs[sample:]
    total = ins[0][...]
    for ref in ins[1:]:
        total = total + ref[...]
    two_ref[...] = total[:own]
    three_ref[...] = total[own : own + times]
    lines = total.shape[0] - own - times
    points = one_ref.shape[1]
    for n in range(one_ref.shape[0] // lines):
        one_ref[n * lines : (n + 1) * lines, :] = total[
            own + times :, n * points : (n + 1) * points
        ]


def on_device(
    ensemble, map_one, map_two, map_three, map_four, core_one, core_two, core_three, core_four
):
    space, sample = lax.axis_size("space"), lax.axis_size("sample")
    times, _, points, _ = ensemble.shape
    rank, width = core_two.shape[1], map_two.shape[1]
    chips = space // 2
    chunks = min(CHUNKS, rank // (space * sample))
    every = range(chunks)

    sent = core_partial(ensemble, core_one, core_two, space, sample, BLOCK, chunks)
    keep, send = sent[:chunks], sent[chunks:]
    got = [swap(s, "space", 1) for s in send]
    stages = core_tree(space, sample)
    ways = len(stages[0])
    rows = keep[0].shape[0] // (chips * ways)
    state = [[keep[k], got[k]] for k in every]
    last = None
    for n, plans in enumerate(stages):
        for k in every:
            after = [] if last is None else [last]
            passed = send if n == 1 and k == chunks - 1 else None
            outs = core_stage(state[k], plans, rows, n == 0, sample, rank, after, passed)
            if passed is not None:
                *outs, send = outs
            last = outs[-1]
            if n + 1 < len(stages):
                state[k] = []
                for way, (_, bit) in enumerate(plans):
                    went, stayed = outs[2 * way : 2 * way + 2]
                    state[k] += [stayed, swap(went, "space", 2 * bit)]
            else:
                state[k] = [swap(p, "sample", far) if far else p for far, p in enumerate(outs)]
        if n == 0:
            mine, send, first = sketch_partial(
                ensemble, map_one, map_two, map_three, map_four, last, space, sample, BLOCK
            )
            last = first
        if n == min(1, len(stages) - 1):
            theirs = swap(send, "space", 1)
            tail = times + 8
            lines = (mine.shape[0] - tail) // chips
            own = lines // sample
            pieces = small_call(
                functools.partial(add_kernel, list(range(chips)), lines, tail),
                [(lines + tail, width)] * chips, "add_cores", [mine, theirs], [last],
            )
            last = pieces[0]
            pieces = [swap(p, "space", 2 * u) if u else p for u, p in enumerate(pieces)]

    total = rank // (space * sample)
    piece = total // chunks
    length = own + times + first.shape[1]
    *pieces, fourth = small_call(
        functools.partial(mix_kernel, sample, own, times, chips),
        [(length, width)] * sample + [(1, width)], "add_chips", [*pieces, first],
    )
    core = None
    for k in every:
        core, _ = final_core(
            state[k], core_three, core_four, [pieces[0]], (0, k * piece, piece, total), core
        )
    pieces = [swap(p, "sample", far) if far else p for far, p in enumerate(pieces)]
    one, two, three = small_call(
        functools.partial(end_kernel, sample, own, times),
        [(width // sample, points), (own, width), (times, width)], "add_samples", pieces,
    )
    return (one.T, two, three, fourth, core)


def solution(mesh):
    placed = (
        P(None, "sample", "space", None),
        P("space", None),
        P(),
        P(),
        P("sample", None),
        P(),
        P(),
        P(),
        P(),
    )
    return jax.shard_map(
        on_device,
        mesh=mesh,
        in_specs=placed,
        out_specs=(
            P("space", "sample"),
            P(("space", "sample"), None),
            P(),
            P("sample", None),
            P(None, ("space", "sample"), None),
        ),
        check_vma=False,
    )
```

```python
import functools

import jax
import jax.numpy as jnp
from jax import lax
from jax.experimental import pallas as pl
from jax.experimental.pallas import tpu as pltpu
from jax.sharding import PartitionSpec as P

BF16 = jnp.bfloat16
F32 = jnp.float32
NT = (((1,), (1,)), ((), ()))
MIB = 1 << 20
CHUNKS = 1
BLOCK, PORTIONS = 4, (2, 4, 6)
SPAN, SLOTS = 4, 4
LIGHT = pl.CostEstimate(flops=1, bytes_accessed=1, transcendentals=0)


def split(value):
    high = value.astype(BF16)
    return high, (value - high.astype(F32)).astype(BF16)


def portions(times, block):
    lengths = [n * block for n in PORTIONS]
    while sum(lengths) < times:
        lengths.append(min(lengths[-1], times - sum(lengths)))
    return lengths


def core_kernel(
    space, sample, block, chunks, x_hbm, two_hbm, one_hbm, *refs
):
    outs, (x_ref, two_ref, one_ref, left_ref, right_ref, sems) = refs[: 2 * chunks], refs[2 * chunks :]
    times, points, _ = x_ref.shape
    rank = two_ref.shape[1]
    half = rank // 2
    count = times // block
    me, my = lax.axis_index("space"), lax.axis_index("sample")
    copies = [
        pltpu.make_async_copy(two_hbm, two_ref, sems.at[count]),
        pltpu.make_async_copy(
            one_hbm.at[pl.ds(pl.multiple_of(me * points, points), points)], one_ref, sems.at[count + 1]
        ),
    ]
    loads = [
        pltpu.make_async_copy(
            x_hbm.at[pl.ds(n * block, block), 0], x_ref.at[pl.ds(n * block, block)], sems.at[n]
        )
        for n in range(count)
    ]
    for copy in copies + loads:
        copy.start()
    own = rank // (space * sample)
    piece = own // chunks
    slot = lax.broadcasted_iota(jnp.int32, (rank, rank), 0)
    column = lax.broadcasted_iota(jnp.int32, (rank, rank), 1)
    odd = slot // half
    rest = slot % half
    part = rest // (half // chunks)
    rest = rest % (half // chunks)
    inner = rest % piece
    far = (rest // piece) % sample
    chip = rest // (piece * sample)
    place = ((chip * 2 + odd) ^ me) * sample + (far ^ my)
    pick = jnp.where(column == place * own + part * piece + inner, 1.0, 0.0).astype(BF16)
    groups = sample
    wide = rank // groups
    row = lax.broadcasted_iota(jnp.int32, (rank, rank), 0)
    group, within = column // wide, column % wide
    source = (within // 2) * (2 * groups) + 2 * group + within % 2
    order = jnp.where(row == source, 1.0, 0.0).astype(BF16)
    for copy in copies:
        copy.wait()
    left_ref[...] = lax.dot_general(
        pick, two_ref[...], NT, preferred_element_type=F32
    ).astype(BF16)
    ordered = jnp.dot(one_ref[...], order, preferred_element_type=F32).astype(BF16)
    right_ref[...] = jnp.concatenate([ordered, ordered], axis=0)

    size = half // chunks
    start = 0
    for length in portions(times, block):
        for n in range(start // block, (start + length) // block):
            loads[n].wait()
        x = x_ref[start : start + length].reshape(length * points, x_ref.shape[2])
        first = lax.dot_general(left_ref[...], x, NT, preferred_element_type=F32)
        rows = []
        for t in range(length):
            high, low = split(first[:, t * points : (t + 1) * points])
            rows.append(jnp.concatenate([high, low], axis=1))
        out = jnp.dot(
            jnp.concatenate(rows, axis=0), right_ref[...], preferred_element_type=F32
        )
        for t in range(length):
            for k in range(2 * chunks):
                at = t * rank + k * size
                outs[k][pl.ds(start + t, size, stride=times), :] = out[at : at + size]
        start += length


def core_partial(ensemble, core_one, core_two, space, sample, block, chunks):
    times, _, points, width = ensemble.shape
    rank = core_two.shape[1]
    shape = jax.ShapeDtypeStruct((rank // 2 // chunks * times, rank), F32)
    hbm = pl.BlockSpec(memory_space=pltpu.HBM)
    return pl.pallas_call(
        functools.partial(core_kernel, space, sample, block, chunks),
        in_specs=[hbm] * 3,
        out_specs=[pl.BlockSpec(memory_space=pltpu.VMEM)] * (2 * chunks),
        out_shape=[shape] * (2 * chunks),
        scratch_shapes=[
            pltpu.VMEM((times, points, width), BF16),
            pltpu.VMEM(core_two.shape, BF16),
            pltpu.VMEM((points, rank), BF16),
            pltpu.VMEM((rank, width), BF16),
            pltpu.VMEM((2 * points, rank), BF16),
            pltpu.SemaphoreType.DMA((times // block + 2,)),
        ],
        compiler_params=pltpu.CompilerParams(vmem_limit_bytes=28 * MIB),
        cost_estimate=LIGHT,
        name="core_partial",
    )(
        pltpu.with_memory_space_constraint(ensemble, pltpu.HBM),
        pltpu.with_memory_space_constraint(core_two, pltpu.HBM),
        pltpu.with_memory_space_constraint(core_one, pltpu.HBM),
    )


def sketch_kernel(
    space, sample, block, x_hbm, one_ref, two_ref, three_ref, four_ref, c_three_ref, c_four_ref, after_ref,
    keep_ref, send_ref, first_ref, final_left_ref, final_base_ref,
    x_ref, acc_one, acc_two, acc_u, pairs, flipped, one_t, turned, sems,
):
    del after_ref
    me, my = lax.axis_index("space"), lax.axis_index("sample")
    times, points, cols = x_ref.shape
    width = two_ref.shape[1]
    count = times // block
    loads = [
        pltpu.make_async_copy(
            x_hbm.at[pl.ds(n * block, block), 0], x_ref.at[pl.ds(n * block, block)], sems.at[n]
        )
        for n in range(count)
    ]
    for load in loads:
        load.start()
    four = four_ref[...].astype(F32)
    pair = three_ref[...].astype(F32) * four
    pairs[...] = pair
    padded = jnp.concatenate([pair, jnp.zeros((128 - times, width), F32)], axis=0)
    flipped[...] = padded.T
    one = one_ref[...].astype(F32)
    if points < 128:
        one = jnp.concatenate([one, jnp.zeros((128 - points, width), F32)], axis=0)
    one_t[...] = one.T[:, :points]
    final_constants(sample, my, c_three_ref, c_four_ref, final_left_ref, final_base_ref)

    start = 0
    for length in portions(times, block):
        for n in range(start // block, (start + length) // block):
            loads[n].wait()
        x = x_ref[start : start + length].reshape(length * points, cols)
        proj = jnp.dot(x, two_ref[...], preferred_element_type=F32)
        one = one_ref[...].astype(F32)
        total = acc_one[...] if start else jnp.zeros_like(acc_one)
        krao = []
        for t in range(length):
            at = start + t
            part = proj[t * points : (t + 1) * points]
            total = total + part * pairs[at : at + 1, :]
            acc_u[at : at + 1, :] = jnp.sum(part * one, axis=0, keepdims=True)
            krao.append((flipped[:, at : at + 1] * one_t[...]).astype(BF16))
        acc_one[...] = total
        more = jnp.dot(jnp.concatenate(krao, axis=1), x, preferred_element_type=F32)
        acc_two[...] = acc_two[...] + more if start else more
        start += length

    turned[...] = acc_two[...].T
    own = cols // (space * sample)
    for slot in range(space):
        ref = send_ref if slot % 2 else keep_ref
        for far in range(sample):
            place = (slot ^ me) * sample + (far ^ my)
            at = (slot // 2 * sample + far) * own
            ref[at : at + own, :] = turned[pl.ds(pl.multiple_of(place * own, own), own), :]
    for ref in (keep_ref, send_ref):
        ref[space // 2 * sample * own :, :] = acc_u[...]
    narrow, folds = width // sample, width // points
    lines = narrow // folds
    square = acc_one[...]
    if points < 128:
        square = jnp.concatenate([square, jnp.zeros((128 - points, width), F32)], axis=0)
    turned[:width, :128] = square.T
    for far in range(sample):
        at = (far ^ my) * narrow
        pieces = [
            turned[pl.ds(pl.multiple_of(at + n * lines, 8), lines), :points] for n in range(folds)
        ]
        first_ref[far] = jnp.concatenate(pieces, axis=1)


def sketch_partial(
    ensemble, map_one, map_two, map_three, map_four, core_three, core_four, after, space, sample, block
):
    times, _, points, cols = ensemble.shape
    width, rank = map_two.shape[1], core_three.shape[1]
    own = cols // (space * sample)
    shape = jax.ShapeDtypeStruct((space // 2 * sample * own + times, width), F32)
    first = jax.ShapeDtypeStruct((sample, points // sample, width), F32)
    anywhere = pl.BlockSpec(memory_space=pl.ANY)
    return pl.pallas_call(
        functools.partial(sketch_kernel, space, sample, block),
        in_specs=[pl.BlockSpec(memory_space=pltpu.HBM)]
        + [pl.BlockSpec(memory_space=pltpu.VMEM)] * 6
        + [anywhere],
        out_specs=[pl.BlockSpec(memory_space=pltpu.VMEM)] * 5,
        out_shape=[
            shape,
            shape,
            first,
            jax.ShapeDtypeStruct((rank, 2 * times), BF16),
            jax.ShapeDtypeStruct((2 * rank, 2 * rank), F32),
        ],
        scratch_shapes=[
            pltpu.VMEM((times, points, cols), BF16),
            pltpu.VMEM((points, width), F32),
            pltpu.VMEM((width, cols), F32),
            pltpu.VMEM((times, width), F32),
            pltpu.VMEM((times, width), F32),
            pltpu.VMEM((width, 128), F32),
            pltpu.VMEM((width, points), F32),
            pltpu.VMEM((cols, width), F32),
            pltpu.SemaphoreType.DMA((times // block,)),
        ],
        compiler_params=pltpu.CompilerParams(vmem_limit_bytes=32 * MIB),
        cost_estimate=LIGHT,
        name="sketch_partial",
    )(
        pltpu.with_memory_space_constraint(ensemble, pltpu.HBM),
        map_one, map_two, map_three, map_four, core_three, core_four, after,
    )


def final_constants(sample, my, three_ref, four_ref, left_ref, base_ref):
    times, rank = three_ref.shape
    wide = rank // sample
    three = three_ref[...].astype(F32)
    three = jnp.concatenate([three, jnp.zeros((rank - times, rank), F32)], axis=0).T
    three = three[:, :times].astype(BF16)
    left_ref[...] = jnp.concatenate([three, three], axis=1)
    four = four_ref[...].astype(F32)
    which = lax.broadcasted_iota(jnp.int32, (sample, rank), 0)
    odd = lax.broadcasted_iota(jnp.int32, (wide, 2 * rank), 0) % 2
    side = lax.broadcasted_iota(jnp.int32, (wide, 2 * rank), 1) // rank
    pieces = []
    for r in range(sample):
        line = jnp.sum(jnp.where(which == (r ^ my), four, 0.0), axis=0, keepdims=True)
        line = jnp.concatenate([line, line], axis=1)
        pieces.append(jnp.where(odd == side, line, 0.0))
    base_ref[...] = jnp.concatenate(pieces * 2, axis=0)


def final_kernel(sample, place, *refs):
    start, first, count, _ = place
    *ins, out_hbm, left_ref, ring, sems = refs
    parts, (three_ref, base_ref) = ins[:sample][::-1], ins[sample : sample + 2]
    rank, times = three_ref.shape[0], three_ref.shape[1] // 2
    wide = rank // sample
    slots, each = ring.shape[0], ring.shape[1]
    step = 2 * sample
    span = each // step
    row = (lax.broadcasted_iota(jnp.int32, base_ref.shape, 0) % wide) // 2

    def copy(b, slot, m, group):
        at = pl.multiple_of((first + b) * rank, rank)
        return pltpu.make_async_copy(
            ring.at[slot, pl.ds(m * step, step)],
            out_hbm.at[pl.ds(group * each + m * step, step), pl.ds(at, rank)],
            sems.at[slot * span + m],
        )

    groups = rank // each

    def block(b):
        held = [
            part[pl.ds(pl.multiple_of((start + b) * times, 8), times), :] for part in parts
        ]
        joined = []
        for g in range(sample):
            joined += [h[:, g * wide : (g + 1) * wide] for h in held]
        high, low = split(jnp.concatenate(joined, axis=1))
        both = jnp.concatenate([high, low], axis=0)
        high, low = split(jnp.dot(three_ref[...], both, preferred_element_type=F32))
        for g in range(sample):
            at = slice(g * rank, (g + 1) * rank)
            left_ref[at, :] = jnp.concatenate([high[:, at], low[:, at]], axis=1)

        def some(n, _):
            for slot in range(slots):
                group = n * slots + slot

                @pl.when((b > 0) | (n > 0))
                def _():
                    for m in range(span):
                        copy(0, slot, m, 0).wait()

                for m in range(span):
                    right = jnp.where(row == group * span + m, base_ref[...], 0.0).astype(BF16)
                    out = jnp.dot(left_ref[...], right, preferred_element_type=F32)
                    for g in range(sample):
                        for k in range(2):
                            ring[slot, m * step + 2 * g + k] = out[
                                g * rank : (g + 1) * rank, k * rank : (k + 1) * rank
                            ]
                    copy(b, slot, m, group).start()

        lax.fori_loop(0, groups // slots, some, None)

    pl.loop(0, count)(block)
    for slot in range(slots):
        for m in range(span):
            copy(0, slot, m, 0).wait()


def final_core(parts, three, base, after, place, into):
    sample = len(parts)
    rank = three.shape[0]
    vmem, anywhere = pl.BlockSpec(memory_space=pltpu.VMEM), pl.BlockSpec(memory_space=pl.ANY)
    extra = list(after) + ([into] if into is not None else [])
    each = min(rank, 2 * sample * SPAN)
    slots = min(SLOTS, rank // each)
    return pl.pallas_call(
        functools.partial(final_kernel, sample, place),
        in_specs=[vmem] * (sample + 2) + [anywhere] * len(extra),
        out_specs=anywhere,
        out_shape=jax.ShapeDtypeStruct((rank, place[3] * rank, rank), F32),
        scratch_shapes=[
            pltpu.VMEM((sample * rank, 2 * rank), BF16),
            pltpu.VMEM((slots, each, rank, rank), F32),
            pltpu.SemaphoreType.DMA((slots * each // (2 * sample),)),
        ],
        input_output_aliases={sample + 1 + len(extra): 0} if into is not None else {},
        compiler_params=pltpu.CompilerParams(vmem_limit_bytes=32 * MIB),
        cost_estimate=pl.CostEstimate(
            flops=4 * rank**4, bytes_accessed=4 * place[2] * rank**3, transcendentals=0
        ),
        name="final_core",
    )(*parts[::-1], three, base, *extra)


def swap(value, axis, mask):
    size = lax.axis_size(axis)
    return lax.ppermute(value, axis, [(i, i ^ mask) for i in range(size)])


def small_call(kernel, outs, name, args, after=()):
    vmem, anywhere = pl.BlockSpec(memory_space=pltpu.VMEM), pl.BlockSpec(memory_space=pl.ANY)
    count = len(args)

    def body(*refs):
        kernel(*refs[:count], *refs[count + len(after) :])

    return pl.pallas_call(
        body,
        in_specs=[vmem] * count + [anywhere] * len(after),
        out_specs=[vmem] * len(outs),
        out_shape=[jax.ShapeDtypeStruct(s, F32) for s in outs],
        compiler_params=pltpu.CompilerParams(vmem_limit_bytes=16 * MIB),
        cost_estimate=LIGHT,
        name=name,
    )(*args, *after)


def route(blocks, bit):
    stay = [u for u in blocks if not u & bit]
    return [u ^ bit for u in stay], stay


def core_kernel_add(rows, first, plans, passed, *refs):
    ways = len(plans)
    count = 2 if first else 2 * ways
    ins, outs = refs[:count], list(refs[count:])
    if passed:
        outs[-1][...] = outs[0][...]
        outs = outs[1:-1]
    for way, (slots, bit) in enumerate(plans):
        stay, came = ins if first else ins[2 * way : 2 * way + 2]

        def total(n):
            u = slots[n]
            at = slice((u * ways + way) * rows, (u * ways + way + 1) * rows)
            if not first:
                at = slice(n * rows, (n + 1) * rows)
            return stay[at, :] + came[at, :]

        if bit:
            for chosen in route(slots, bit):
                out = outs.pop(0)
                for n, u in enumerate(chosen):
                    out[n * rows : (n + 1) * rows, :] = total(slots.index(u))
        else:
            value = total(0)
            each = outs[0].shape[0]
            for n in range(rows // each):
                outs.pop(0)[...] = value[n * each : (n + 1) * each]


def core_stage(values, plans, rows, first, sample, rank, after, passed=None):
    ways = len(plans)
    shapes = []
    for slots, bit in plans:
        if bit:
            shapes += [(len(slots) // 2 * rows, rank)] * 2
        else:
            shapes += [(rows // (sample // ways), rank)] * (sample // ways)
    if passed is not None:
        values, shapes = [*values, passed], [*shapes, passed.shape]
    return small_call(
        functools.partial(core_kernel_add, rows, first, plans, passed is not None),
        shapes, "add_core", values, after,
    )


def core_tree(space, sample):
    chips = space // 2
    bits = [1 << n for n in range(chips.bit_length() - 1)]
    ways = 2 if len(bits) > 1 and sample % 2 == 0 else 1
    orders = [bits[way:] + bits[:way] for way in range(ways)]
    held = [list(range(chips)) for _ in range(ways)]
    stages = []
    for n in range(len(bits) + 1):
        plans = []
        for way in range(ways):
            bit = orders[way][n] if n < len(bits) else 0
            plans.append((held[way], bit))
            if bit:
                held[way] = route(held[way], bit)[1]
        stages.append(plans)
    return stages


def add_kernel(blocks, rows, tail, *refs):
    keep_ref, got_ref, *outs = refs
    at = keep_ref.shape[0] - tail
    end = keep_ref[at:, :] + got_ref[at:, :]
    for u, out in zip(blocks, outs):
        at = slice(u * rows, (u + 1) * rows)
        out[:rows, :] = keep_ref[at, :] + got_ref[at, :]
        out[rows:, :] = end


def mix_kernel(sample, own, count, *refs):
    ins, (first_ref, three_ref, four_ref), outs = refs[:count][::-1], refs[count : count + 3], refs[count + 3 :]
    *outs, fourth_ref = outs
    total = ins[0][...]
    for ref in ins[1:]:
        total = total + ref[...]
    times = three_ref.shape[0]
    u = total[sample * own :]
    third = u * four_ref[...].astype(F32)
    for far in range(sample):
        outs[far][:own, :] = total[far * own : (far + 1) * own]
        outs[far][own : own + times, :] = third
        outs[far][own + times :, :] = first_ref[far]
    fourth_ref[...] = jnp.sum(u * three_ref[...].astype(F32), axis=0, keepdims=True)


def end_kernel(sample, own, times, *refs):
    ins, (mid_ref, one_ref, two_ref, three_ref, four_ref) = refs[:sample], refs[sample:]
    four_ref[...] = mid_ref[...]
    total = ins[0][...]
    for ref in ins[1:]:
        total = total + ref[...]
    two_ref[...] = total[:own]
    three_ref[...] = total[own : own + times]
    lines = total.shape[0] - own - times
    points = one_ref.shape[1]
    for n in range(one_ref.shape[0] // lines):
        one_ref[n * lines : (n + 1) * lines, :] = total[
            own + times :, n * points : (n + 1) * points
        ]


def on_device(
    ensemble, map_one, map_two, map_three, map_four, core_one, core_two, core_three, core_four
):
    space, sample = lax.axis_size("space"), lax.axis_size("sample")
    times, _, points, _ = ensemble.shape
    rank, width = core_two.shape[1], map_two.shape[1]
    chips = space // 2
    chunks = min(CHUNKS, rank // (space * sample))
    every = range(chunks)

    sent = core_partial(ensemble, core_one, core_two, space, sample, BLOCK, chunks)
    keep, send = sent[:chunks], sent[chunks:]
    got = [swap(s, "space", 1) for s in send]
    stages = core_tree(space, sample)
    ways = len(stages[0])
    rows = keep[0].shape[0] // (chips * ways)
    state = [[keep[k], got[k]] for k in every]
    last = None
    for n, plans in enumerate(stages):
        for k in every:
            after = [] if last is None else [last]
            passed = send if n == 1 and k == chunks - 1 else None
            outs = core_stage(state[k], plans, rows, n == 0, sample, rank, after, passed)
            if passed is not None:
                *outs, send = outs
            last = outs[-1]
            if n + 1 < len(stages):
                state[k] = []
                for way, (_, bit) in enumerate(plans):
                    went, stayed = outs[2 * way : 2 * way + 2]
                    state[k] += [stayed, swap(went, "space", 2 * bit)]
            else:
                state[k] = [swap(p, "sample", far) if far else p for far, p in enumerate(outs)]
        if n == 0:
            mine, send, first, turned, base = sketch_partial(
                ensemble, map_one, map_two, map_three, map_four, core_three, core_four, last,
                space, sample, BLOCK,
            )
            last = first
        if n == min(1, len(stages) - 1):
            theirs = swap(send, "space", 1)
            lines = (mine.shape[0] - times) // chips
            own = lines // sample
            pieces = small_call(
                functools.partial(add_kernel, list(range(chips)), lines, times),
                [(lines + times, width)] * chips, "add_cores", [mine, theirs], [last],
            )
            last = pieces[0]
            pieces = [swap(p, "space", 2 * u) if u else p for u, p in enumerate(pieces)]

    total = rank // (space * sample)
    piece = total // chunks
    length = own + times + first.shape[1]
    *pieces, fourth = small_call(
        functools.partial(mix_kernel, sample, own, chips),
        [(length, width)] * sample + [(1, width)], "add_chips",
        [*pieces[::-1], first, map_three, map_four],
    )
    core = None
    for k in every:
        core = final_core(state[k], turned, base, [pieces[0]], (0, k * piece, piece, total), core)
    pieces = [swap(p, "sample", far) if far else p for far, p in enumerate(pieces)]
    one, two, three, fourth = small_call(
        functools.partial(end_kernel, sample, own, times),
        [(width // sample, points), (own, width), (times, width), (1, width)], "add_samples",
        [*pieces, fourth],
    )
    return (one.T, two, three, fourth, core)


def solution(mesh):
    placed = (
        P(None, "sample", "space", None),
        P("space", None),
        P(),
        P(),
        P("sample", None),
        P(),
        P(),
        P(),
        P(),
    )
    return jax.shard_map(
        on_device,
        mesh=mesh,
        in_specs=placed,
        out_specs=(
            P("space", "sample"),
            P(("space", "sample"), None),
            P(),
            P("sample", None),
            P(None, ("space", "sample"), None),
        ),
        check_vma=False,
    )
```

```python
import functools

import jax
import jax.numpy as jnp
from jax import lax
from jax.experimental import pallas as pl
from jax.experimental.pallas import tpu as pltpu
from jax.sharding import PartitionSpec as P

BF16 = jnp.bfloat16
F32 = jnp.float32
NT = (((1,), (1,)), ((), ()))
MIB = 1 << 20
CHUNKS = 1
BLOCK, PORTIONS = 4, (2, 4, 6)
SPAN, SLOTS = 4, 4
LIGHT = pl.CostEstimate(flops=1, bytes_accessed=1, transcendentals=0)


def split(value):
    high = value.astype(BF16)
    return high, (value - high.astype(F32)).astype(BF16)


def portions(times, block):
    lengths = [n * block for n in PORTIONS]
    while sum(lengths) < times:
        lengths.append(min(lengths[-1], times - sum(lengths)))
    return lengths


def core_kernel(
    space, sample, block, chunks, x_hbm, two_hbm, one_hbm, *refs
):
    outs, (x_ref, two_ref, one_ref, left_ref, right_ref, sems) = refs[: 2 * chunks], refs[2 * chunks :]
    times, points, _ = x_ref.shape
    rank = two_ref.shape[1]
    half = rank // 2
    count = times // block
    me, my = lax.axis_index("space"), lax.axis_index("sample")
    copies = [
        pltpu.make_async_copy(two_hbm, two_ref, sems.at[count]),
        pltpu.make_async_copy(
            one_hbm.at[pl.ds(pl.multiple_of(me * points, points), points)], one_ref, sems.at[count + 1]
        ),
    ]
    loads = [
        pltpu.make_async_copy(
            x_hbm.at[pl.ds(n * block, block), 0], x_ref.at[pl.ds(n * block, block)], sems.at[n]
        )
        for n in range(count)
    ]
    for copy in copies + loads:
        copy.start()
    own = rank // (space * sample)
    piece = own // chunks
    slot = lax.broadcasted_iota(jnp.int32, (rank, rank), 0)
    column = lax.broadcasted_iota(jnp.int32, (rank, rank), 1)
    odd = slot // half
    rest = slot % half
    part = rest // (half // chunks)
    rest = rest % (half // chunks)
    inner = rest % piece
    far = (rest // piece) % sample
    chip = rest // (piece * sample)
    place = ((chip * 2 + odd) ^ me) * sample + (far ^ my)
    pick = jnp.where(column == place * own + part * piece + inner, 1.0, 0.0).astype(BF16)
    groups = sample
    wide = rank // groups
    row = lax.broadcasted_iota(jnp.int32, (rank, rank), 0)
    group, within = column // wide, column % wide
    source = (within // 2) * (2 * groups) + 2 * group + within % 2
    order = jnp.where(row == source, 1.0, 0.0).astype(BF16)
    for copy in copies:
        copy.wait()
    left_ref[...] = lax.dot_general(
        pick, two_ref[...], NT, preferred_element_type=F32
    ).astype(BF16)
    ordered = jnp.dot(one_ref[...], order, preferred_element_type=F32).astype(BF16)
    right_ref[...] = jnp.concatenate([ordered, ordered], axis=0)

    size = half // chunks
    start = 0
    for length in portions(times, block):
        for n in range(start // block, (start + length) // block):
            loads[n].wait()
        x = x_ref[start : start + length].reshape(length * points, x_ref.shape[2])
        first = lax.dot_general(left_ref[...], x, NT, preferred_element_type=F32)
        rows = []
        for t in range(length):
            high, low = split(first[:, t * points : (t + 1) * points])
            rows.append(jnp.concatenate([high, low], axis=1))
        out = jnp.dot(
            jnp.concatenate(rows, axis=0), right_ref[...], preferred_element_type=F32
        )
        for t in range(length):
            for k in range(2 * chunks):
                at = t * rank + k * size
                outs[k][pl.ds(start + t, size, stride=times), :] = out[at : at + size]
        start += length


def core_partial(ensemble, core_one, core_two, space, sample, block, chunks):
    times, _, points, width = ensemble.shape
    rank = core_two.shape[1]
    shape = jax.ShapeDtypeStruct((rank // 2 // chunks * times, rank), F32)
    hbm = pl.BlockSpec(memory_space=pltpu.HBM)
    return pl.pallas_call(
        functools.partial(core_kernel, space, sample, block, chunks),
        in_specs=[hbm] * 3,
        out_specs=[pl.BlockSpec(memory_space=pltpu.VMEM)] * (2 * chunks + 1),
        out_shape=[shape] * (2 * chunks) + [pltpu.VMEM((times, points, width), BF16)],
        scratch_shapes=[
            pltpu.VMEM(core_two.shape, BF16),
            pltpu.VMEM((points, rank), BF16),
            pltpu.VMEM((rank, width), BF16),
            pltpu.VMEM((2 * points, rank), BF16),
            pltpu.SemaphoreType.DMA((times // block + 2,)),
        ],
        compiler_params=pltpu.CompilerParams(vmem_limit_bytes=28 * MIB),
        cost_estimate=LIGHT,
        name="core_partial",
    )(
        pltpu.with_memory_space_constraint(ensemble, pltpu.HBM),
        pltpu.with_memory_space_constraint(core_two, pltpu.HBM),
        pltpu.with_memory_space_constraint(core_one, pltpu.HBM),
    )


def sketch_kernel(
    space, sample, block, x_ref, one_ref, two_ref, three_ref, four_ref, c_three_ref, c_four_ref, after_ref,
    keep_ref, send_ref, first_ref, final_left_ref, final_base_ref,
    acc_one, acc_two, acc_u, pairs, flipped, one_t, turned,
):
    del after_ref
    me, my = lax.axis_index("space"), lax.axis_index("sample")
    times, points, cols = x_ref.shape
    width = two_ref.shape[1]
    four = four_ref[...].astype(F32)
    pair = three_ref[...].astype(F32) * four
    pairs[...] = pair
    padded = jnp.concatenate([pair, jnp.zeros((128 - times, width), F32)], axis=0)
    flipped[...] = padded.T
    one = one_ref[...].astype(F32)
    if points < 128:
        one = jnp.concatenate([one, jnp.zeros((128 - points, width), F32)], axis=0)
    one_t[...] = one.T[:, :points]
    final_constants(sample, my, c_three_ref, c_four_ref, final_left_ref, final_base_ref)

    start = 0
    for length in portions(times, block):
        x = x_ref[start : start + length].reshape(length * points, cols)
        proj = jnp.dot(x, two_ref[...], preferred_element_type=F32)
        one = one_ref[...].astype(F32)
        total = acc_one[...] if start else jnp.zeros_like(acc_one)
        krao = []
        for t in range(length):
            at = start + t
            part = proj[t * points : (t + 1) * points]
            total = total + part * pairs[at : at + 1, :]
            acc_u[at : at + 1, :] = jnp.sum(part * one, axis=0, keepdims=True)
            krao.append((flipped[:, at : at + 1] * one_t[...]).astype(BF16))
        acc_one[...] = total
        more = jnp.dot(jnp.concatenate(krao, axis=1), x, preferred_element_type=F32)
        acc_two[...] = acc_two[...] + more if start else more
        start += length

    turned[...] = acc_two[...].T
    own = cols // (space * sample)
    for slot in range(space):
        ref = send_ref if slot % 2 else keep_ref
        for far in range(sample):
            place = (slot ^ me) * sample + (far ^ my)
            at = (slot // 2 * sample + far) * own
            ref[at : at + own, :] = turned[pl.ds(pl.multiple_of(place * own, own), own), :]
    for ref in (keep_ref, send_ref):
        ref[space // 2 * sample * own :, :] = acc_u[...]
    narrow, folds = width // sample, width // points
    lines = narrow // folds
    square = acc_one[...]
    if points < 128:
        square = jnp.concatenate([square, jnp.zeros((128 - points, width), F32)], axis=0)
    turned[:width, :128] = square.T
    for far in range(sample):
        at = (far ^ my) * narrow
        pieces = [
            turned[pl.ds(pl.multiple_of(at + n * lines, 8), lines), :points] for n in range(folds)
        ]
        first_ref[far] = jnp.concatenate(pieces, axis=1)


def sketch_partial(
    held, map_one, map_two, map_three, map_four, core_three, core_four, after, space, sample, block
):
    times, points, cols = held.shape
    width, rank = map_two.shape[1], core_three.shape[1]
    own = cols // (space * sample)
    shape = jax.ShapeDtypeStruct((space // 2 * sample * own + times, width), F32)
    first = jax.ShapeDtypeStruct((sample, points // sample, width), F32)
    anywhere = pl.BlockSpec(memory_space=pl.ANY)
    return pl.pallas_call(
        functools.partial(sketch_kernel, space, sample, block),
        in_specs=[pl.BlockSpec(memory_space=pltpu.VMEM)] * 7 + [anywhere],
        out_specs=[pl.BlockSpec(memory_space=pltpu.VMEM)] * 5,
        out_shape=[
            pltpu.VMEM(shape.shape, F32),
            pltpu.VMEM(shape.shape, F32),
            pltpu.VMEM(first.shape, F32),
            pltpu.VMEM((rank, 2 * times), BF16),
            pltpu.VMEM((2 * rank, 2 * rank), F32),
        ],
        scratch_shapes=[
            pltpu.VMEM((points, width), F32),
            pltpu.VMEM((width, cols), F32),
            pltpu.VMEM((times, width), F32),
            pltpu.VMEM((times, width), F32),
            pltpu.VMEM((width, 128), F32),
            pltpu.VMEM((width, points), F32),
            pltpu.VMEM((cols, width), F32),
        ],
        compiler_params=pltpu.CompilerParams(vmem_limit_bytes=32 * MIB),
        cost_estimate=LIGHT,
        name="sketch_partial",
    )(
        pltpu.with_memory_space_constraint(held, pltpu.VMEM),
        map_one, map_two, map_three, map_four, core_three, core_four, after,
    )


def final_constants(sample, my, three_ref, four_ref, left_ref, base_ref):
    times, rank = three_ref.shape
    wide = rank // sample
    three = three_ref[...].astype(F32)
    three = jnp.concatenate([three, jnp.zeros((rank - times, rank), F32)], axis=0).T
    three = three[:, :times].astype(BF16)
    left_ref[...] = jnp.concatenate([three, three], axis=1)
    four = four_ref[...].astype(F32)
    which = lax.broadcasted_iota(jnp.int32, (sample, rank), 0)
    odd = lax.broadcasted_iota(jnp.int32, (wide, 2 * rank), 0) % 2
    side = lax.broadcasted_iota(jnp.int32, (wide, 2 * rank), 1) // rank
    pieces = []
    for r in range(sample):
        line = jnp.sum(jnp.where(which == (r ^ my), four, 0.0), axis=0, keepdims=True)
        line = jnp.concatenate([line, line], axis=1)
        pieces.append(jnp.where(odd == side, line, 0.0))
    base_ref[...] = jnp.concatenate(pieces * 2, axis=0)


def final_kernel(sample, place, *refs):
    start, first, count, _ = place
    *ins, out_hbm, left_ref, ring, sems = refs
    parts, (three_ref, base_ref) = ins[:sample][::-1], ins[sample : sample + 2]
    rank, times = three_ref.shape[0], three_ref.shape[1] // 2
    wide = rank // sample
    slots, each = ring.shape[0], ring.shape[1]
    step = 2 * sample
    span = each // step
    row = (lax.broadcasted_iota(jnp.int32, base_ref.shape, 0) % wide) // 2

    def copy(b, slot, m, group):
        at = pl.multiple_of((first + b) * rank, rank)
        return pltpu.make_async_copy(
            ring.at[slot, pl.ds(m * step, step)],
            out_hbm.at[pl.ds(group * each + m * step, step), pl.ds(at, rank)],
            sems.at[slot * span + m],
        )

    groups = rank // each

    def block(b):
        held = [
            part[pl.ds(pl.multiple_of((start + b) * times, 8), times), :] for part in parts
        ]
        joined = []
        for g in range(sample):
            joined += [h[:, g * wide : (g + 1) * wide] for h in held]
        high, low = split(jnp.concatenate(joined, axis=1))
        both = jnp.concatenate([high, low], axis=0)
        high, low = split(jnp.dot(three_ref[...], both, preferred_element_type=F32))
        for g in range(sample):
            at = slice(g * rank, (g + 1) * rank)
            left_ref[at, :] = jnp.concatenate([high[:, at], low[:, at]], axis=1)

        def some(n, _):
            for slot in range(slots):
                group = n * slots + slot

                @pl.when((b > 0) | (n > 0))
                def _():
                    for m in range(span):
                        copy(0, slot, m, 0).wait()

                for m in range(span):
                    right = jnp.where(row == group * span + m, base_ref[...], 0.0).astype(BF16)
                    out = jnp.dot(left_ref[...], right, preferred_element_type=F32)
                    for g in range(sample):
                        for k in range(2):
                            ring[slot, m * step + 2 * g + k] = out[
                                g * rank : (g + 1) * rank, k * rank : (k + 1) * rank
                            ]
                    copy(b, slot, m, group).start()

        lax.fori_loop(0, groups // slots, some, None)

    pl.loop(0, count)(block)
    for slot in range(slots):
        for m in range(span):
            copy(0, slot, m, 0).wait()


def final_core(parts, three, base, after, place, into):
    sample = len(parts)
    rank = three.shape[0]
    vmem, anywhere = pl.BlockSpec(memory_space=pltpu.VMEM), pl.BlockSpec(memory_space=pl.ANY)
    extra = list(after) + ([into] if into is not None else [])
    each = min(rank, 2 * sample * SPAN)
    slots = min(SLOTS, rank // each)
    return pl.pallas_call(
        functools.partial(final_kernel, sample, place),
        in_specs=[vmem] * (sample + 2) + [anywhere] * len(extra),
        out_specs=anywhere,
        out_shape=jax.ShapeDtypeStruct((rank, place[3] * rank, rank), F32),
        scratch_shapes=[
            pltpu.VMEM((sample * rank, 2 * rank), BF16),
            pltpu.VMEM((slots, each, rank, rank), F32),
            pltpu.SemaphoreType.DMA((slots * each // (2 * sample),)),
        ],
        input_output_aliases={sample + 1 + len(extra): 0} if into is not None else {},
        compiler_params=pltpu.CompilerParams(vmem_limit_bytes=32 * MIB),
        cost_estimate=pl.CostEstimate(
            flops=4 * rank**4, bytes_accessed=4 * place[2] * rank**3, transcendentals=0
        ),
        name="final_core",
    )(*parts[::-1], three, base, *extra)


def swap(value, axis, mask):
    size = lax.axis_size(axis)
    return lax.ppermute(value, axis, [(i, i ^ mask) for i in range(size)])


def small_call(kernel, outs, name, args, after=()):
    vmem, anywhere = pl.BlockSpec(memory_space=pltpu.VMEM), pl.BlockSpec(memory_space=pl.ANY)
    count = len(args)

    def body(*refs):
        kernel(*refs[:count], *refs[count + len(after) :])

    return pl.pallas_call(
        body,
        in_specs=[vmem] * count + [anywhere] * len(after),
        out_specs=[vmem] * len(outs),
        out_shape=[jax.ShapeDtypeStruct(s, F32) for s in outs],
        compiler_params=pltpu.CompilerParams(vmem_limit_bytes=16 * MIB),
        cost_estimate=LIGHT,
        name=name,
    )(*args, *after)


def route(blocks, bit):
    stay = [u for u in blocks if not u & bit]
    return [u ^ bit for u in stay], stay


def core_kernel_add(rows, first, plans, passed, *refs):
    ways = len(plans)
    count = 2 if first else 2 * ways
    ins, outs = refs[:count], list(refs[count:])
    if passed:
        outs[-1][...] = outs[0][...]
        outs = outs[1:-1]
    for way, (slots, bit) in enumerate(plans):
        stay, came = ins if first else ins[2 * way : 2 * way + 2]

        def total(n):
            u = slots[n]
            at = slice((u * ways + way) * rows, (u * ways + way + 1) * rows)
            if not first:
                at = slice(n * rows, (n + 1) * rows)
            return stay[at, :] + came[at, :]

        if bit:
            for chosen in route(slots, bit):
                out = outs.pop(0)
                for n, u in enumerate(chosen):
                    out[n * rows : (n + 1) * rows, :] = total(slots.index(u))
        else:
            value = total(0)
            each = outs[0].shape[0]
            for n in range(rows // each):
                outs.pop(0)[...] = value[n * each : (n + 1) * each]


def core_stage(values, plans, rows, first, sample, rank, after, passed=None):
    ways = len(plans)
    shapes = []
    for slots, bit in plans:
        if bit:
            shapes += [(len(slots) // 2 * rows, rank)] * 2
        else:
            shapes += [(rows // (sample // ways), rank)] * (sample // ways)
    if passed is not None:
        values, shapes = [*values, passed], [*shapes, passed.shape]
    return small_call(
        functools.partial(core_kernel_add, rows, first, plans, passed is not None),
        shapes, "add_core", values, after,
    )


def core_tree(space, sample):
    chips = space // 2
    bits = [1 << n for n in range(chips.bit_length() - 1)]
    ways = 2 if len(bits) > 1 and sample % 2 == 0 else 1
    orders = [bits[way:] + bits[:way] for way in range(ways)]
    held = [list(range(chips)) for _ in range(ways)]
    stages = []
    for n in range(len(bits) + 1):
        plans = []
        for way in range(ways):
            bit = orders[way][n] if n < len(bits) else 0
            plans.append((held[way], bit))
            if bit:
                held[way] = route(held[way], bit)[1]
        stages.append(plans)
    return stages


def add_kernel(blocks, rows, tail, *refs):
    keep_ref, got_ref, *outs = refs
    at = keep_ref.shape[0] - tail
    end = keep_ref[at:, :] + got_ref[at:, :]
    for u, out in zip(blocks, outs):
        at = slice(u * rows, (u + 1) * rows)
        out[:rows, :] = keep_ref[at, :] + got_ref[at, :]
        out[rows:, :] = end


def mix_kernel(sample, own, count, *refs):
    ins, (first_ref, three_ref, four_ref), outs = refs[:count][::-1], refs[count : count + 3], refs[count + 3 :]
    *outs, fourth_ref = outs
    total = ins[0][...]
    for ref in ins[1:]:
        total = total + ref[...]
    times = three_ref.shape[0]
    u = total[sample * own :]
    third = u * four_ref[...].astype(F32)
    for far in range(sample):
        outs[far][:own, :] = total[far * own : (far + 1) * own]
        outs[far][own : own + times, :] = third
        outs[far][own + times :, :] = first_ref[far]
    fourth_ref[...] = jnp.sum(u * three_ref[...].astype(F32), axis=0, keepdims=True)


def end_kernel(sample, own, times, *refs):
    ins, (mid_ref, one_ref, two_ref, three_ref, four_ref) = refs[:sample], refs[sample:]
    four_ref[...] = mid_ref[...]
    total = ins[0][...]
    for ref in ins[1:]:
        total = total + ref[...]
    two_ref[...] = total[:own]
    three_ref[...] = total[own : own + times]
    lines = total.shape[0] - own - times
    points = one_ref.shape[1]
    for n in range(one_ref.shape[0] // lines):
        one_ref[n * lines : (n + 1) * lines, :] = total[
            own + times :, n * points : (n + 1) * points
        ]


def on_device(
    ensemble, map_one, map_two, map_three, map_four, core_one, core_two, core_three, core_four
):
    space, sample = lax.axis_size("space"), lax.axis_size("sample")
    times, _, points, _ = ensemble.shape
    rank, width = core_two.shape[1], map_two.shape[1]
    chips = space // 2
    chunks = min(CHUNKS, rank // (space * sample))
    every = range(chunks)

    *sent, held = core_partial(ensemble, core_one, core_two, space, sample, BLOCK, chunks)
    keep, send = sent[:chunks], sent[chunks:]
    got = [swap(s, "space", 1) for s in send]
    stages = core_tree(space, sample)
    ways = len(stages[0])
    rows = keep[0].shape[0] // (chips * ways)
    state = [[keep[k], got[k]] for k in every]
    last = None
    for n, plans in enumerate(stages):
        for k in every:
            after = [] if last is None else [last]
            passed = send if n == 1 and k == chunks - 1 else None
            outs = core_stage(state[k], plans, rows, n == 0, sample, rank, after, passed)
            if passed is not None:
                *outs, send = outs
            last = outs[-1]
            if n + 1 < len(stages):
                state[k] = []
                for way, (_, bit) in enumerate(plans):
                    went, stayed = outs[2 * way : 2 * way + 2]
                    state[k] += [stayed, swap(went, "space", 2 * bit)]
            else:
                state[k] = [swap(p, "sample", far) if far else p for far, p in enumerate(outs)]
        if n == 0:
            mine, send, first, turned, base = sketch_partial(
                held, map_one, map_two, map_three, map_four, core_three, core_four, last,
                space, sample, BLOCK,
            )
            last = first
        if n == min(1, len(stages) - 1):
            theirs = swap(send, "space", 1)
            lines = (mine.shape[0] - times) // chips
            own = lines // sample
            pieces = small_call(
                functools.partial(add_kernel, list(range(chips)), lines, times),
                [(lines + times, width)] * chips, "add_cores", [mine, theirs], [last],
            )
            last = pieces[0]
            pieces = [swap(p, "space", 2 * u) if u else p for u, p in enumerate(pieces)]

    total = rank // (space * sample)
    piece = total // chunks
    length = own + times + first.shape[1]
    *pieces, fourth = small_call(
        functools.partial(mix_kernel, sample, own, chips),
        [(length, width)] * sample + [(1, width)], "add_chips",
        [*pieces[::-1], first, map_three, map_four],
    )
    core = None
    for k in every:
        core = final_core(state[k], turned, base, [pieces[0]], (0, k * piece, piece, total), core)
    pieces = [swap(p, "sample", far) if far else p for far, p in enumerate(pieces)]
    one, two, three, fourth = small_call(
        functools.partial(end_kernel, sample, own, times),
        [(width // sample, points), (own, width), (times, width), (1, width)], "add_samples",
        [*pieces, fourth],
    )
    return (one.T, two, three, fourth, core)


def solution(mesh):
    placed = (
        P(None, "sample", "space", None),
        P("space", None),
        P(),
        P(),
        P("sample", None),
        P(),
        P(),
        P(),
        P(),
    )
    return jax.shard_map(
        on_device,
        mesh=mesh,
        in_specs=placed,
        out_specs=(
            P("space", "sample"),
            P(("space", "sample"), None),
            P(),
            P("sample", None),
            P(None, ("space", "sample"), None),
        ),
        check_vma=False,
    )
```
